256 devices in a mesh: dp: 16 (over z_lo, x), mp: 16 (over z_hi, y, core).
Axes of the slice: x: 4, y: 4, z: 8 (z_hi: 2, z_lo: 4; z = z_hi * 4 + z_lo), core: 2. Of those that a mesh axis runs over, the one named last changes fastest.
Arguments:
- field: bfloat16 [16, 32, 128, 64, 128], P('dp', None, 'mp'), may hold values from -6 to 6
- cotangent: bfloat16 [16, 32, 128, 64, 128], P('dp', None, 'mp'), may hold values from -6 to 6
- spectral_weight: float32 [32, 32, 32, 32, 32], P('mp', 'dp'), may hold values from -6 to 6
- first_moment: float32 [32, 32, 32, 32, 32], P('mp', 'dp'), may hold values from -4.2 to 4.2
- second_moment: float32 [32, 32, 32, 32, 32], P('mp', 'dp'), may hold values from 4 to 64
- local_weight: bfloat16 [32, 32], replicated, may hold values from -1 to 1
Outputs:
- new_weight: float32 [32, 32, 32, 32, 32], P('mp', 'dp')
- new_first: float32 [32, 32, 32, 32, 32], P('mp', 'dp')
- new_second: float32 [32, 32, 32, 32, 32], P('mp', 'dp')
The draws below stay inside these ranges and needn't reach their ends.
All inputs are finite; a program needn't handle non-finite values.
Results may differ from the reference program's by a relative error of at most 0.02.
Values may be sent and summed in bfloat16 or wider, within the bound.
No kernel may reach another device: no remote copies, remote signals or barrier semaphores. Data moves between devices by JAX's collectives and lax.ppermute only.
A program may use at most 192 MiB of HBM per device.

```python
import math
import jax
import jax.numpy as jnp
from jax import lax

C = 32
NX = 64
NY = 128
NZ = 128
KM = 16
K2 = 32
B = 16


def block_scale(own_key, dims, cuts, least, top_value):
    level = 1.0
    for position, shards_of in cuts:
        steps = jax.random.uniform(jax.random.fold_in(jax.random.fold_in(own_key, 6), position), (shards_of,), jnp.float32, least / len(cuts), top_value / len(cuts))
        level = level * jnp.repeat(jnp.exp(steps), dims[position] // shards_of).reshape((-1,) + (1,) * (len(dims) - 1 - position))
    return level


def scatter_about(own_key, extent, width, limit, split=(), kind=jnp.bfloat16):
    entries = width * jax.random.normal(own_key, extent, jnp.float32)
    if split:
        entries = entries * block_scale(own_key, extent, split, -0.22, 0.18)
    return jnp.clip(entries, -limit, limit).astype(kind)


def setup_inputs(seed: int = 0) -> dict:
    key_of = jax.random.split(jax.random.key(seed), 7)
    return {
        "field": scatter_about(key_of[0], (B, C, NZ, NX, NY), 1.0, 6.0, ((0, 16), (2, 16))),
        "cotangent": scatter_about(key_of[1], (B, C, NZ, NX, NY), 1.0, 6.0, ((0, 16), (2, 16))),
        "spectral_weight": scatter_about(key_of[2], (K2, K2, K2, C, C), (max(1, C * K2 * K2 * K2 // (NX * NY * NZ))) ** -0.5, 6.0, ((0, 16), (1, 16)), jnp.float32),
        "first_moment": scatter_about(key_of[3], (K2, K2, K2, C, C), 0.7, 4.2, ((0, 16), (1, 16)), jnp.float32),
        "second_moment": jnp.clip(jnp.exp(math.log(64.0) - 2.7725887 * jax.random.uniform(key_of[4], (K2, K2, K2, C, C), jnp.float32) ** block_scale(key_of[4], (K2, K2, K2, C, C), ((0, 16), (1, 16)), -0.2, 0.2)), 4.0, 64.0),
        "local_weight": scatter_about(key_of[5], (C, C), C ** -0.5, 1.0),
    }


beta_one = 0.9
beta_two = 0.999
learn_rate = 0.001
decay_rate = 0.1
adam_eps = 1e-08
adam_step = 1000.0

def table(length, modes):
    grid = jnp.arange(length, dtype=jnp.float32)[:, None]
    index = jnp.arange(2 * modes, dtype=jnp.float32)[None, :]
    freq = jnp.where(index < modes, index, index - modes + 1.0)
    phase = 2.0 * jnp.pi * freq * grid / length
    values = jnp.where(index < modes, jnp.cos(phase), jnp.sin(phase)) * jnp.sqrt(2.0 / length)
    return values.astype(jnp.bfloat16)

def project_onto_modes(draw_example, cosine_sine_x_table, cosine_sine_y_table, cosine_sine_z_table):
    first = jnp.einsum('czxy,yb->czxb', draw_example.astype(jnp.float32), cosine_sine_y_table.astype(jnp.float32)).astype(jnp.bfloat16)
    second = jnp.einsum('czxb,xa->czab', first.astype(jnp.float32), cosine_sine_x_table.astype(jnp.float32)).astype(jnp.bfloat16)
    return jnp.einsum('czab,zk->cabk', second.astype(jnp.float32), cosine_sine_z_table.astype(jnp.float32)).astype(jnp.bfloat16)

def from_modes(coeffs, cosine_sine_x_table, cosine_sine_y_table, cosine_sine_z_table):
    first = jnp.einsum('cabk,zk->czab', coeffs.astype(jnp.float32), cosine_sine_z_table.astype(jnp.float32)).astype(jnp.bfloat16)
    second = jnp.einsum('czab,xa->czxb', first.astype(jnp.float32), cosine_sine_x_table.astype(jnp.float32)).astype(jnp.bfloat16)
    return jnp.einsum('czxb,yb->czxy', second.astype(jnp.float32), cosine_sine_y_table.astype(jnp.float32))

def reference(field, cotangent, spectral_weight, first_moment, second_moment, local_weight):
    cosine_sine_x_table = table(NX, KM)
    cosine_sine_y_table = table(NY, KM)
    cosine_sine_z_table = table(NZ, KM)
    input_spectrum = lax.map(lambda draw_example: project_onto_modes(draw_example, cosine_sine_x_table, cosine_sine_y_table, cosine_sine_z_table), field)
    lowest_mode_weight = spectral_weight.astype(jnp.bfloat16)
    output_spectrum = jnp.einsum('wrydf,ydfrn->wnydf', input_spectrum.astype(jnp.float32), lowest_mode_weight.astype(jnp.float32)).astype(jnp.bfloat16)

    def backward_one(items):
        draw_example, cot, coeffs = items
        spectral = from_modes(coeffs, cosine_sine_x_table, cosine_sine_y_table, cosine_sine_z_table)
        local = jnp.einsum('czxy,co->ozxy', draw_example.astype(jnp.float32), local_weight.astype(jnp.float32))
        pre = spectral + local
        unused, pull = jax.vjp(jax.nn.gelu, pre)
        grad_pre = pull(cot.astype(pre.dtype))[0].astype(jnp.bfloat16)
        return project_onto_modes(grad_pre, cosine_sine_x_table, cosine_sine_y_table, cosine_sine_z_table)
    gradient_spectrum = lax.map(backward_one, (field, cotangent, output_spectrum))
    weight_gradient = jnp.einsum('upghz,utghz->ghzpt', input_spectrum.astype(jnp.float32), gradient_spectrum.astype(jnp.float32))
    new_first = beta_one * first_moment + (1.0 - beta_one) * weight_gradient
    new_second = beta_two * second_moment + (1.0 - beta_two) * weight_gradient * weight_gradient
    first_hat = new_first / (1.0 - beta_one ** adam_step)
    second_hat = new_second / (1.0 - beta_two ** adam_step)
    new_weight = spectral_weight - learn_rate * (first_hat / (jnp.sqrt(second_hat) + adam_eps) + decay_rate * spectral_weight)
    return (new_weight, new_first, new_second)
```

```python
import jax
import jax.numpy as jnp
import ml_dtypes
import numpy as np
from jax import lax
from jax.experimental import pallas as pl
from jax.experimental.pallas import tpu as pltpu
from jax.sharding import PartitionSpec as P

beta_one = 0.9
beta_two = 0.999
learn_rate = 0.001
decay_rate = 0.1
adam_eps = 1e-08
adam_step = 1000.0

F32 = jnp.float32
BF16 = jnp.bfloat16
VMEM = 40 * 1024 * 1024


def table(length, modes=16):
    grid = np.arange(length, dtype=np.float32)[:, None]
    index = np.arange(2 * modes, dtype=np.float32)[None, :]
    freq = np.where(index < modes, index, index - np.float32(modes - 1)).astype(np.float32)
    phase = (np.float32(2.0 * np.pi) * freq * grid / np.float32(length)).astype(np.float32)
    values = np.where(index < modes, np.cos(phase), np.sin(phase)) * np.sqrt(np.float32(2.0 / length))
    return values.astype(np.float32).astype(ml_dtypes.bfloat16).astype(np.float32)


def constants():
    bx, by, bz = table(64), table(128), table(128)
    left_x = np.einsum("xa,cd->acdx", bx, np.eye(8, dtype=np.float32)).reshape(256, 512)
    by_rows = by.T.reshape(16, 2, 128).transpose(1, 0, 2).reshape(32, 128)
    by_blocks = np.kron(np.eye(4, dtype=np.float32), by_rows)
    left_z = np.einsum(
        "nqtk,bd->btkndq", bz.reshape(16, 4, 2, 32), np.eye(2, dtype=np.float32)
    ).reshape(128, 128)
    low = lambda v: jnp.asarray(np.ascontiguousarray(v).astype(ml_dtypes.bfloat16))
    return low(left_x), low(left_x.T), low(by_rows), low(by_blocks), low(left_z), low(left_z.T)


def dot(a, b):
    return lax.dot_general(a, b, (((1,), (0,)), ((), ())), preferred_element_type=F32)


def dot_nt(a, b):
    return lax.dot_general(a, b, (((1,), (1,)), ((), ())), preferred_element_type=F32)


def whole(shape):
    zeros = (0,) * len(shape)
    return pl.BlockSpec(shape, lambda i: zeros)


def call(kernel, grid, in_specs, out_specs, out_shape, scratch, flops, name):
    return pl.pallas_call(
        kernel,
        grid=(grid,),
        in_specs=in_specs,
        out_specs=out_specs,
        out_shape=out_shape,
        scratch_shapes=scratch,
        compiler_params=pltpu.CompilerParams(vmem_limit_bytes=VMEM),
        cost_estimate=pl.CostEstimate(flops=flops, bytes_accessed=8 << 20, transcendentals=0),
        name=name,
    )


def store_x_modes(first, group, product):
    split = product.reshape(16, 2, 8, 256)
    for z2 in range(2):
        first[:, z2, :, group] = split[:, :, :, z2 * 128 : (z2 + 1) * 128]


def y_modes_to_messages(first, by_rows, messages, zq):
    rows = first[...].reshape(2048, 128).astype(BF16)
    planar = dot_nt(by_rows, rows)
    for ap in range(16):
        for b2 in range(2):
            messages[pl.ds(ap * 8 + b2 * 4 + zq, 16, stride=128), :] = planar[
                b2 * 16 : (b2 + 1) * 16, ap * 128 : (ap + 1) * 128
            ]


def forward_kernel(field, left_x, by_rows, out, first, messages):
    zq = pl.program_id(0)
    for group in range(4):
        block = jnp.concatenate(
            [field[0, group * 8 : (group + 1) * 8, z2].reshape(512, 128) for z2 in range(2)], axis=1
        )
        store_x_modes(first, group, dot(left_x[...], block))
    y_modes_to_messages(first, by_rows[...], messages, zq)

    @pl.when(zq == 3)
    def _():
        out[...] = messages[...].astype(BF16)


def forward(field, left_x, by_rows):
    return call(
        forward_kernel,
        4,
        [
            pl.BlockSpec((1, 32, 2, 64, 128), lambda i: (0, 0, i, 0, 0)),
            whole((256, 512)),
            whole((32, 128)),
        ],
        whole((2048, 128)),
        jax.ShapeDtypeStruct((2048, 128), BF16),
        [pltpu.VMEM((16, 2, 2, 4, 8, 128), F32), pltpu.VMEM((2048, 128), F32)],
        1 << 31,
        "planes_to_modes",
    )(field, left_x, by_rows)


def local_kernel(field, left_c, out):
    for xg in range(4):
        cols = []
        for z2 in range(2):
            rows = field[0, :, z2, xg * 16 : (xg + 1) * 16, :].astype(F32)
            cols.append(rows.reshape(32, 2, 8, 128))
        halves = []
        for half in range(2):
            block = jnp.concatenate([c[:, half].reshape(256, 128) for c in cols], axis=1)
            halves.append(dot(left_c[...], block.astype(BF16)))
        for z2 in range(2):
            parts = [h[:, z2 * 128 : (z2 + 1) * 128].reshape(32, 1, 8, 128) for h in halves]
            both = jnp.concatenate(parts, axis=1).reshape(32, 16, 128)
            out[0, :, z2, xg * 16 : (xg + 1) * 16, :] = both.astype(BF16)


def local_mix(field, left_c):
    plane = pl.BlockSpec((1, 32, 2, 64, 128), lambda i: (0, 0, i, 0, 0))
    return call(
        local_kernel,
        4,
        [plane, whole((256, 256))],
        plane,
        jax.ShapeDtypeStruct(field.shape, BF16),
        [],
        1 << 31,
        "local_mix",
    )(field, left_c)


def spread_kernel(weight, out):
    row = lax.broadcasted_iota(jnp.int32, (32, 128), 0)
    lane = lax.broadcasted_iota(jnp.int32, (32, 128), 1)
    for b2 in range(2):
        for a2 in range(2):
            r = b2 * 2 + a2
            shift = jnp.where(lane == row + 32 * r, 1.0, 0.0).astype(BF16)
            rows = weight[a2, b2].reshape(256, 32).astype(BF16)
            out[:, r * 32 : (r + 1) * 32, :] = dot(rows, shift).astype(BF16).reshape(8, 32, 128)


def spread_weights(weight):
    return call(
        spread_kernel,
        4,
        [pl.BlockSpec((2, 2, 8, 32, 32), lambda i: (0, 0, i, 0, 0))],
        pl.BlockSpec((8, 128, 128), lambda i: (i, 0, 0)),
        jax.ShapeDtypeStruct((32, 128, 128), BF16),
        [],
        1 << 28,
        "spread_weights",
    )(weight)


def z_modes(received, left_z, spectrum):
    low_half = lax.broadcasted_iota(jnp.int32, (32, 128), 1) < 64
    for s in range(16):
        p = dot(left_z, received[s * 128 : (s + 1) * 128, :])
        stay = jnp.where(low_half, p[0:32], p[96:128])
        move = jnp.where(low_half, p[64:96], p[32:64])
        spectrum[pl.ds(s, 32, stride=16), :] = stay + pltpu.roll(move, 64, axis=1)


def mix_kernel(received, weights, left_z, right_z, out, kept, spectrum, mixed):
    z_modes(received, left_z[...], spectrum)
    kept[...] = spectrum[...].astype(BF16)
    for k in range(32):
        rows = slice(k * 16, (k + 1) * 16)
        mixed[rows, :] = dot(spectrum[rows, :].astype(BF16), weights[k])
    low_half = lax.broadcasted_iota(jnp.int32, (32, 128), 1) < 64
    for s in range(16):
        y = mixed[pl.ds(s, 32, stride=16), :]
        turned = pltpu.roll(y, 64, axis=1)
        stack = [
            jnp.where(low_half, y, 0.0),
            jnp.where(low_half, 0.0, turned),
            jnp.where(low_half, turned, 0.0),
            jnp.where(low_half, 0.0, y),
        ]
        block = jnp.concatenate(stack, axis=0).astype(BF16)
        out[s * 128 : (s + 1) * 128, :] = dot(right_z[...], block).astype(BF16)


def mix(received, weights, left_z, right_z):
    return call(
        mix_kernel,
        1,
        [whole((2048, 128)), whole((32, 128, 128)), whole((128, 128)), whole((128, 128))],
        [whole((2048, 128)), whole((512, 128))],
        [jax.ShapeDtypeStruct((2048, 128), BF16), jax.ShapeDtypeStruct((512, 128), BF16)],
        [pltpu.VMEM((512, 128), F32), pltpu.VMEM((512, 128), F32)],
        1 << 28,
        "mix_modes",
    )(received, weights, left_z, right_z)


def gelu_slope(v):
    k = 0.7978845608028654
    square = v * v
    t = jnp.tanh(v * (square * (k * 0.044715) + k))
    slope = v * (square * (3.0 * k * 0.044715) + k)
    return (1.0 + t) + (1.0 - t * t) * slope


def middle_kernel(received, local, cot, left_x, right_x, by_rows, by_blocks, out, planes, depth, first, messages):
    zq = pl.program_id(0)

    @pl.when(zq == 0)
    def _():
        planes[...] = received[...].astype(F32)

    for apg in range(4):
        rows = [
            planes[pl.ds((apg * 4 + j) * 8 + b2 * 4 + zq, 16, stride=128), :]
            for j in range(4)
            for b2 in range(2)
        ]
        turned = jnp.concatenate(rows, axis=0).T.astype(BF16)
        product = dot(turned, by_blocks[...])
        for j in range(4):
            depth[apg * 4 + j] = product[:, j * 128 : (j + 1) * 128].reshape(2, 2, 4, 8, 128)

    for group in range(4):
        block = jnp.concatenate(
            [depth[:, z2, :, group].reshape(256, 128).astype(BF16) for z2 in range(2)], axis=1
        )
        pre = dot(right_x[...], block)
        grads = []
        for z2 in range(2):
            rows = slice(group * 8, (group + 1) * 8)
            v = pre[:, z2 * 128 : (z2 + 1) * 128] + local[0, rows, z2].reshape(512, 128).astype(F32)
            c = 0.5 * cot[0, rows, z2].reshape(512, 128).astype(F32)
            grads.append((c * gelu_slope(v)).astype(BF16))
        store_x_modes(first, group, dot(left_x[...], jnp.concatenate(grads, axis=1)))
    y_modes_to_messages(first, by_rows[...], messages, zq)

    @pl.when(zq == 3)
    def _():
        out[...] = messages[...].astype(BF16)


def middle(received, local, cot, left_x, right_x, by_rows, by_blocks):
    plane = pl.BlockSpec((1, 32, 2, 64, 128), lambda i: (0, 0, i, 0, 0))
    return call(
        middle_kernel,
        4,
        [
            whole((2048, 128)),
            plane,
            plane,
            whole((256, 512)),
            whole((512, 256)),
            whole((32, 128)),
            whole((128, 512)),
        ],
        whole((2048, 128)),
        jax.ShapeDtypeStruct((2048, 128), BF16),
        [
            pltpu.VMEM((2048, 128), F32),
            pltpu.VMEM((16, 2, 2, 4, 8, 128), F32),
            pltpu.VMEM((16, 2, 2, 4, 8, 128), F32),
            pltpu.VMEM((2048, 128), F32),
        ],
        1 << 32,
        "gelu_gradient",
    )(received, local, cot, left_x, right_x, by_rows, by_blocks)


def update_kernel(received, kept, left_z, weight, moment, second, new_weight, new_moment, new_second, spectrum):
    step = pl.program_id(0)

    @pl.when(step == 0)
    def _():
        z_modes(received, left_z[...], spectrum)

    start = pl.multiple_of(step * 128, 128)
    left = kept[pl.ds(start, 128), :].astype(F32).T.astype(BF16)
    right = spectrum[pl.ds(start, 128), :].astype(BF16)
    zero = jnp.zeros((16, 128), BF16)
    columns = []
    for k in range(8):
        tiles = [zero] * 8
        tiles[k] = right[k * 16 : (k + 1) * 16]
        columns.append(jnp.concatenate(tiles, axis=0))
    product = dot(left, jnp.concatenate(columns, axis=1))
    for k in range(8):
        for b2 in range(2):
            for a2 in range(2):
                r = b2 * 2 + a2
                block = product[r * 32 : (r + 1) * 32, k * 128 : (k + 1) * 128]
                if r:
                    block = pltpu.roll(block, 128 - 32 * r, axis=1)
                grad = block[:, :32]
                w = weight[a2, b2, k]
                first = beta_one * moment[a2, b2, k] + (1.0 - beta_one) * grad
                square = beta_two * second[a2, b2, k] + (1.0 - beta_two) * grad * grad
                first_hat = first / (1.0 - beta_one**adam_step)
                second_hat = square / (1.0 - beta_two**adam_step)
                new_moment[a2, b2, k] = first
                new_second[a2, b2, k] = square
                new_weight[a2, b2, k] = w - learn_rate * (
                    first_hat / (jnp.sqrt(second_hat) + adam_eps) + decay_rate * w
                )


def update(received, kept, left_z, weight, moment, second):
    block = pl.BlockSpec((2, 2, 8, 32, 32), lambda i: (0, 0, i, 0, 0))
    return call(
        update_kernel,
        4,
        [whole((2048, 128)), whole((512, 128)), whole((128, 128)), block, block, block],
        [block] * 3,
        [jax.ShapeDtypeStruct(weight.shape, F32)] * 3,
        [pltpu.VMEM((512, 128), F32)],
        1 << 28,
        "adam_update",
    )(received, kept, left_z, weight, moment, second)


def exchange(messages):
    return lax.all_to_all(messages, ("dp", "mp"), split_axis=0, concat_axis=0, tiled=True)


def body(field, cotangent, spectral_weight, first_moment, second_moment, local_weight):
    left_x, right_x, by_rows, by_blocks, left_z, right_z = constants()
    eye = jnp.eye(8, dtype=BF16)
    left_c = (local_weight.T[:, None, :, None] * eye[None, :, None, :]).reshape(256, 256)
    received = exchange(forward(field, left_x, by_rows))
    local = local_mix(field, left_c)
    spread = spread_weights(spectral_weight)
    mixed, kept = mix(received, spread, left_z, right_z)
    received = exchange(mixed)
    received = exchange(middle(received, local, cotangent, left_x, right_x, by_rows, by_blocks))
    return tuple(update(received, kept, left_z, spectral_weight, first_moment, second_moment))


def solution(mesh):
    spread = P("dp", None, "mp", None, None)
    modes = P("mp", "dp", None, None, None)
    return jax.shard_map(
        body,
        mesh=mesh,
        in_specs=(spread, spread, modes, modes, modes, P()),
        out_specs=(modes, modes, modes),
        check_vma=False,
    )
```

```python
import jax
import jax.numpy as jnp
import ml_dtypes
import numpy as np
from jax import lax
from jax.experimental import pallas as pl
from jax.experimental.pallas import tpu as pltpu
from jax.sharding import PartitionSpec as P

beta_one = 0.9
beta_two = 0.999
learn_rate = 0.001
decay_rate = 0.1
adam_eps = 1e-08
adam_step = 1000.0

F32 = jnp.float32
BF16 = jnp.bfloat16
MIB = 1024 * 1024


def table(length, modes=16):
    grid = np.arange(length, dtype=np.float32)[:, None]
    index = np.arange(2 * modes, dtype=np.float32)[None, :]
    freq = np.where(index < modes, index, index - np.float32(modes - 1)).astype(np.float32)
    phase = (np.float32(2.0 * np.pi) * freq * grid / np.float32(length)).astype(np.float32)
    values = np.where(index < modes, np.cos(phase), np.sin(phase)) * np.sqrt(np.float32(2.0 / length))
    return values.astype(np.float32).astype(ml_dtypes.bfloat16).astype(np.float32)


def constants():
    bx, by, bz = table(64), table(128), table(128)
    left_x = np.einsum("xa,cd->acdx", bx, np.eye(4)).reshape(128, 256)
    right_x = np.einsum("xpt,cd,gh->gcxphtd", bx.reshape(64, 16, 2), np.eye(4), np.eye(2)).reshape(512, 256)
    right_y = np.einsum("yb,qr->qybr", by, np.eye(4)).reshape(512, 128)
    left_z = np.einsum("nqtk,bd->btkndq", bz.reshape(16, 4, 2, 32), np.eye(2)).reshape(128, 128)
    order = np.eye(128).reshape(2, 2, 8, 4, 128).transpose(0, 2, 1, 3, 4).reshape(128, 128).T
    low = lambda v: jnp.asarray(np.ascontiguousarray(v).astype(ml_dtypes.bfloat16))
    left_y = right_y.T
    tables = (left_x, right_x, left_y, left_y * 0.5, left_z, left_z.T, order, order.T)
    return [low(v) for v in tables]


def dot(a, b):
    return lax.dot_general(a, b, (((1,), (0,)), ((), ())), preferred_element_type=F32)


def dot_nt(a, b):
    return lax.dot_general(a, b, (((1,), (1,)), ((), ())), preferred_element_type=F32)


def whole(shape):
    zeros = (0,) * len(shape)
    return pl.BlockSpec(shape, lambda i: zeros)


def resident():
    return pl.BlockSpec(memory_space=pltpu.VMEM)


def call(kernel, grid, in_specs, out_specs, out_shape, scratch, flops, name, vmem):
    return pl.pallas_call(
        kernel,
        grid=(grid,),
        in_specs=in_specs,
        out_specs=out_specs,
        out_shape=out_shape,
        scratch_shapes=scratch,
        compiler_params=pltpu.CompilerParams(vmem_limit_bytes=vmem * MIB),
        cost_estimate=pl.CostEstimate(flops=flops, bytes_accessed=8 << 20, transcendentals=0),
        name=name,
    )


def store_x_modes(first, left_x, zq, group, planes):
    halves = []
    for half in range(2):
        rows = slice(half * 256, (half + 1) * 256)
        block = jnp.concatenate([p[rows] for p in planes], axis=1)
        halves.append(dot(left_x, block).reshape(16, 1, 8, 256))
    both = jnp.concatenate(halves, axis=1).reshape(16, 16, 256).astype(BF16)
    for z2 in range(2):
        first[:, zq, z2, group] = both[:, :, z2 * 128 : (z2 + 1) * 128]


def store_messages(first, left_y, out):
    for pair in range(8):
        planes = [first[pair * 2 : pair * 2 + 2, zq].reshape(256, 128) for zq in range(4)]
        planar = dot_nt(left_y, jnp.concatenate(planes, axis=1))
        tiles = [planar[:, :128].reshape(16, 8, 128), planar[:, 128:].reshape(16, 8, 128)]
        out[:, pair] = jnp.concatenate(tiles, axis=1).astype(BF16)


def forward_kernel(field, left_x, left_y, out, first):
    zq = pl.program_id(0)
    for group in range(4):
        planes = [field[0, group * 8 : (group + 1) * 8, z2].reshape(512, 128) for z2 in range(2)]
        store_x_modes(first, left_x[...], zq, group, planes)

    @pl.when(zq == 3)
    def _():
        store_messages(first, left_y[...], out)


FIRST = (16, 4, 2, 4, 16, 128)
MESSAGES = (16, 8, 16, 128)


def forward(field, left_x, left_y):
    return call(
        forward_kernel,
        4,
        [
            pl.BlockSpec((1, 32, 2, 64, 128), lambda i: (0, 0, i, 0, 0)),
            whole((128, 256)),
            whole((128, 512)),
        ],
        whole(MESSAGES),
        jax.ShapeDtypeStruct(MESSAGES, BF16),
        [pltpu.VMEM(FIRST, BF16)],
        1 << 31,
        "planes_to_modes",
        60,
    )(field, left_x, left_y).reshape(2048, 128)


def local_kernel(field, left_c, out):
    for xg in range(4):
        cols = []
        for z2 in range(2):
            rows = field[0, :, z2, xg * 16 : (xg + 1) * 16, :].astype(F32)
            cols.append(rows.reshape(32, 2, 8, 128))
        halves = []
        for half in range(2):
            block = jnp.concatenate([c[:, half].reshape(256, 128) for c in cols], axis=1)
            halves.append(dot(left_c[...], block.astype(BF16)))
        for z2 in range(2):
            parts = [h[:, z2 * 128 : (z2 + 1) * 128].reshape(32, 1, 8, 128) for h in halves]
            both = jnp.concatenate(parts, axis=1).reshape(32, 16, 128)
            out[0, :, z2, xg * 16 : (xg + 1) * 16, :] = both.astype(BF16)


def local_mix(field, left_c):
    plane = pl.BlockSpec((1, 32, 2, 64, 128), lambda i: (0, 0, i, 0, 0))
    return call(
        local_kernel,
        4,
        [plane, whole((256, 256))],
        plane,
        jax.ShapeDtypeStruct(field.shape, BF16),
        [],
        1 << 31,
        "local_mix",
        24,
    )(field, left_c)


def spread_kernel(weight, order, order_t, out):
    rows = []
    for b2 in range(2):
        for a2 in range(2):
            r = b2 * 2 + a2
            flat = weight[a2, b2].reshape(256, 32).astype(BF16)
            rows.append(dot(flat, order[r * 32 : (r + 1) * 32, :]).astype(BF16))
    for k in range(8):
        block = jnp.concatenate([v[k * 32 : (k + 1) * 32] for v in rows], axis=0)
        out[k] = dot(order_t[...], block).astype(BF16)


def spread_weights(weight, order, order_t):
    return call(
        spread_kernel,
        4,
        [pl.BlockSpec((2, 2, 8, 32, 32), lambda i: (0, 0, i, 0, 0)), whole((128, 128)), whole((128, 128))],
        pl.BlockSpec((8, 128, 128), lambda i: (i, 0, 0)),
        jax.ShapeDtypeStruct((32, 128, 128), BF16),
        [],
        1 << 28,
        "spread_weights",
        16,
    )(weight, order, order_t)


def z_modes(received, left_z, spectrum):
    low_half = lax.broadcasted_iota(jnp.int32, (32, 128), 1) < 64
    for pair in range(8):
        both = [received[s * 128 : (s + 1) * 128, :] for s in (2 * pair, 2 * pair + 1)]
        product = dot(left_z, jnp.concatenate(both, axis=1))
        for odd in range(2):
            p = product[:, odd * 128 : (odd + 1) * 128]
            stay = jnp.where(low_half, p[0:32], p[96:128])
            move = jnp.where(low_half, p[64:96], p[32:64])
            spectrum[pl.ds(2 * pair + odd, 32, stride=16), :] = stay + pltpu.roll(move, 64, axis=1)


def mix_kernel(received, weights, left_z, right_z, out, kept, spectrum, mixed):
    z_modes(received, left_z[...], spectrum)
    kept[...] = spectrum[...].astype(BF16)
    for k in range(32):
        rows = slice(k * 16, (k + 1) * 16)
        mixed[rows, :] = dot(spectrum[rows, :].astype(BF16), weights[k])
    low_half = lax.broadcasted_iota(jnp.int32, (32, 128), 1) < 64
    for pair in range(8):
        blocks = []
        for s in (2 * pair, 2 * pair + 1):
            y = mixed[pl.ds(s, 32, stride=16), :]
            turned = pltpu.roll(y, 64, axis=1)
            stack = [
                jnp.where(low_half, y, 0.0),
                jnp.where(low_half, 0.0, turned),
                jnp.where(low_half, turned, 0.0),
                jnp.where(low_half, 0.0, y),
            ]
            blocks.append(jnp.concatenate(stack, axis=0).astype(BF16))
        product = dot(right_z[...], jnp.concatenate(blocks, axis=1)).astype(BF16)
        for odd in range(2):
            s = 2 * pair + odd
            out[s * 128 : (s + 1) * 128, :] = product[:, odd * 128 : (odd + 1) * 128]


def mix(received, weights, left_z, right_z):
    return call(
        mix_kernel,
        1,
        [whole((2048, 128)), whole((32, 128, 128)), whole((128, 128)), whole((128, 128))],
        [whole((2048, 128)), whole((512, 128))],
        [jax.ShapeDtypeStruct((2048, 128), BF16), jax.ShapeDtypeStruct((512, 128), BF16)],
        [pltpu.VMEM((512, 128), F32), pltpu.VMEM((512, 128), F32)],
        1 << 34,
        "mix_modes",
        16,
    )(received, weights, left_z, right_z)


def gelu_pull(v, cot):
    k = 0.7978845608028654
    square = v * v
    t = jnp.tanh(v * (square * low(k * 0.044715) + low(k)))
    slope = v * (square * low(3.0 * k * 0.044715) + low(k))
    one = low(1.0)
    return cot * ((one + t) * (one + (one - t) * slope))


def low(value):
    return jnp.asarray(value, BF16)


def middle_kernel(received, local, cot, left_x, right_x, left_y, half_y, out, depth, first, spectral):
    turned = []
    for pair in range(8):
        both = received[:, pair].astype(F32).reshape(16, 2, 8, 128)
        for odd in range(2):
            turned.append(both[:, odd].reshape(128, 128).T.astype(BF16))
    product = dot(jnp.concatenate(turned, axis=0), left_y[...]).astype(BF16)
    for zq in range(4):
        depth[zq] = product[:, zq * 128 : (zq + 1) * 128].reshape(16, 2, 4, 16, 128)

    def inverse(zq, group):
        block = jnp.concatenate([depth[zq, :, z2, group].reshape(256, 128) for z2 in range(2)], axis=1)
        spectral[group % 2] = dot(right_x[...], block).astype(BF16)

    def quarter(zq, carry):
        inverse(zq, 0)
        for group in range(4):
            if group < 3:
                inverse(zq, group + 1)
            planes = []
            for z2 in range(2):
                rows = slice(group * 8, (group + 1) * 8)
                v = spectral[group % 2, :, z2 * 128 : (z2 + 1) * 128]
                v = v + local[0, rows, zq * 2 + z2].reshape(512, 128)
                planes.append(gelu_pull(v, cot[0, rows, zq * 2 + z2].reshape(512, 128)))
            store_x_modes(first, left_x[...], zq, group, planes)
        return carry

    lax.fori_loop(0, 4, quarter, 0)
    store_messages(first, half_y[...], out)


def middle(received, local, cot, left_x, right_x, left_y, half_y):
    return call(
        middle_kernel,
        1,
        [
            whole(MESSAGES),
            resident(),
            resident(),
            whole((128, 256)),
            whole((512, 256)),
            whole((128, 512)),
            whole((128, 512)),
        ],
        whole(MESSAGES),
        jax.ShapeDtypeStruct(MESSAGES, BF16),
        [
            pltpu.VMEM((4, 16, 2, 4, 16, 128), BF16),
            pltpu.VMEM(FIRST, BF16),
            pltpu.VMEM((2, 512, 256), BF16),
        ],
        1 << 32,
        "gelu_gradient",
        32,
    )(received.reshape(MESSAGES), local, cot, left_x, right_x, left_y, half_y).reshape(2048, 128)


def update_kernel(received, kept, left_z, order_t, weight, moment, second, new_weight, new_moment, new_second, spectrum):
    step = pl.program_id(0)

    @pl.when(step == 0)
    def _():
        z_modes(received, left_z[...], spectrum)

    start = pl.multiple_of(step * 128, 128)
    left = dot(kept[pl.ds(start, 128), :], order_t[...]).T.astype(BF16)
    right = dot(spectrum[pl.ds(start, 128), :].astype(BF16), order_t[...]).astype(BF16)
    zero = jnp.zeros((16, 128), BF16)
    columns = []
    for k in range(8):
        tiles = [zero] * 8
        tiles[k] = right[k * 16 : (k + 1) * 16]
        columns.append(jnp.concatenate(tiles, axis=0))
    product = dot(left, jnp.concatenate(columns, axis=1))
    for k in range(8):
        for b2 in range(2):
            for a2 in range(2):
                r = b2 * 2 + a2
                block = product[r * 32 : (r + 1) * 32, k * 128 : (k + 1) * 128]
                if r:
                    block = pltpu.roll(block, 128 - 32 * r, axis=1)
                grad = block[:, :32]
                w = weight[a2, b2, step * 8 + k]
                first = beta_one * moment[a2, b2, step * 8 + k] + (1.0 - beta_one) * grad
                square = beta_two * second[a2, b2, step * 8 + k] + (1.0 - beta_two) * grad * grad
                first_hat = first / (1.0 - beta_one**adam_step)
                second_hat = square / (1.0 - beta_two**adam_step)
                new_moment[a2, b2, k] = first
                new_second[a2, b2, k] = square
                new_weight[a2, b2, k] = w - learn_rate * (
                    first_hat / (jnp.sqrt(second_hat) + adam_eps) + decay_rate * w
                )


def update(received, kept, left_z, order_t, weight, moment, second):
    block = pl.BlockSpec((2, 2, 8, 32, 32), lambda i: (0, 0, i, 0, 0))
    return call(
        update_kernel,
        4,
        [whole((2048, 128)), whole((512, 128)), whole((128, 128)), whole((128, 128)), resident(), resident(), resident()],
        [block] * 3,
        [jax.ShapeDtypeStruct(weight.shape, F32)] * 3,
        [pltpu.VMEM((512, 128), F32)],
        1 << 28,
        "adam_update",
        24,
    )(received, kept, left_z, order_t, weight, moment, second)


def exchange(messages):
    return lax.all_to_all(messages, ("dp", "mp"), split_axis=0, concat_axis=0, tiled=True)


def body(field, cotangent, spectral_weight, first_moment, second_moment, local_weight):
    left_x, right_x, left_y, half_y, left_z, right_z, order, order_t = constants()
    eye = jnp.eye(8, dtype=BF16)
    left_c = (local_weight.T[:, None, :, None] * eye[None, :, None, :]).reshape(256, 256)
    received = exchange(forward(field, left_x, left_y))
    local = local_mix(field, left_c)
    spread = spread_weights(spectral_weight, order, order_t)
    received, local, spread = lax.optimization_barrier((received, local, spread))
    mixed, kept = mix(received, spread, left_z, right_z)
    received = exchange(mixed)
    received = exchange(middle(received, local, cotangent, left_x, right_x, left_y, half_y))
    return tuple(update(received, kept, left_z, order_t, spectral_weight, first_moment, second_moment))


def solution(mesh):
    spread = P("dp", None, "mp", None, None)
    modes = P("mp", "dp", None, None, None)
    return jax.shard_map(
        body,
        mesh=mesh,
        in_specs=(spread, spread, modes, modes, modes, P()),
        out_specs=(modes, modes, modes),
        check_vma=False,
    )
```

```python
import jax
import jax.numpy as jnp
import ml_dtypes
import numpy as np
from jax import lax
from jax.experimental import pallas as pl
from jax.experimental.pallas import tpu as pltpu
from jax.sharding import PartitionSpec as P

beta_one = 0.9
beta_two = 0.999
learn_rate = 0.001
decay_rate = 0.1
adam_eps = 1e-08
adam_step = 1000.0

F32 = jnp.float32
BF16 = jnp.bfloat16
MIB = 1024 * 1024


def table(length, modes=16):
    grid = np.arange(length, dtype=np.float32)[:, None]
    index = np.arange(2 * modes, dtype=np.float32)[None, :]
    freq = np.where(index < modes, index, index - np.float32(modes - 1)).astype(np.float32)
    phase = (np.float32(2.0 * np.pi) * freq * grid / np.float32(length)).astype(np.float32)
    values = np.where(index < modes, np.cos(phase), np.sin(phase)) * np.sqrt(np.float32(2.0 / length))
    return values.astype(np.float32).astype(ml_dtypes.bfloat16).astype(np.float32)


def constants():
    bx, by, bz = table(64), table(128), table(128)
    left_x = np.einsum("xa,cd->acdx", bx, np.eye(4)).reshape(128, 256)
    right_y = np.einsum("yb,qr->qybr", by, np.eye(4)).reshape(512, 128)
    left_z = np.einsum("nqtk,bd->btkndq", bz.reshape(16, 4, 2, 32), np.eye(2)).reshape(128, 128)
    order = np.eye(128).reshape(2, 2, 8, 4, 128).transpose(0, 2, 1, 3, 4).reshape(128, 128).T
    low = lambda v: jnp.asarray(np.ascontiguousarray(v).astype(ml_dtypes.bfloat16))
    tables = (left_x, left_x.T, left_x * 0.5, right_y, right_y.T, left_z, left_z.T, order, order.T)
    return [low(v) for v in tables]


def dot(a, b):
    return lax.dot_general(a, b, (((1,), (0,)), ((), ())), preferred_element_type=F32)


def dot_nt(a, b):
    return lax.dot_general(a, b, (((1,), (1,)), ((), ())), preferred_element_type=F32)


def whole(shape):
    zeros = (0,) * len(shape)
    return pl.BlockSpec(shape, lambda i: zeros)


def resident():
    return pl.BlockSpec(memory_space=pltpu.VMEM)


def outside():
    return pl.BlockSpec(memory_space=pl.ANY)


def call(kernel, grid, in_specs, out_specs, out_shape, scratch, flops, name, vmem):
    return pl.pallas_call(
        kernel,
        grid=(grid,),
        in_specs=in_specs,
        out_specs=out_specs,
        out_shape=out_shape,
        scratch_shapes=scratch,
        compiler_params=pltpu.CompilerParams(vmem_limit_bytes=vmem * MIB),
        cost_estimate=pl.CostEstimate(flops=flops, bytes_accessed=8 << 20, transcendentals=0),
        name=name,
    )


def store_modes(planar, right_y, left_x, start, planes):
    zero = jnp.zeros((512, 128), BF16)
    both = jnp.concatenate(
        [jnp.concatenate([right_y, zero], axis=1), jnp.concatenate([zero, right_y], axis=1)], axis=0
    )
    modes = dot(jnp.concatenate(planes, axis=1), both).astype(BF16)
    for i in range(modes.shape[0] // 256):
        product = dot(left_x, modes[i * 256 : (i + 1) * 256]).reshape(16, 8, 256)
        for z2 in range(2):
            planar[:, z2, start + i] = product[:, :, z2 * 128 : (z2 + 1) * 128]


def store_messages(planar, out):
    for pair in range(8):
        tiles = [planar[ap].reshape(128, 128).T.reshape(16, 8, 128) for ap in (pair * 2, pair * 2 + 1)]
        out[:, pair] = jnp.concatenate(tiles, axis=1).astype(BF16)


def forward_kernel(field, left_x, right_y, out, planar):
    step = pl.program_id(0)
    planes = [field[0, :, zq * 2 + z2].reshape(512, 128) for z2 in range(2) for zq in range(4)]
    store_modes(planar, right_y[...], left_x[...], step * 2, planes)

    @pl.when(step == 3)
    def _():
        store_messages(planar, out)


PLANAR = (16, 2, 8, 8, 128)
MESSAGES = (16, 8, 16, 128)


def forward(field, left_x, right_y):
    return call(
        forward_kernel,
        4,
        [
            pl.BlockSpec((1, 8, 8, 64, 128), lambda i: (0, i, 0, 0, 0)),
            whole((128, 256)),
            whole((512, 128)),
        ],
        whole(MESSAGES),
        jax.ShapeDtypeStruct(MESSAGES, BF16),
        [pltpu.VMEM(PLANAR, F32)],
        1 << 31,
        "planes_to_modes",
        60,
    )(field, left_x, right_y).reshape(2048, 128)


def local_kernel(field, weight, out, left_c):
    @pl.when(pl.program_id(0) == 0)
    def _():
        row = lax.broadcasted_iota(jnp.int32, (256, 32), 0)
        column = lax.broadcasted_iota(jnp.int32, (256, 32), 1)
        spread = jnp.where(row // 8 == column, 1.0, 0.0).astype(BF16)
        rows = dot_nt(spread, weight[...]).astype(BF16)
        row = lax.broadcasted_iota(jnp.int32, (256, 256), 0)
        column = lax.broadcasted_iota(jnp.int32, (256, 256), 1)
        left_c[...] = jnp.where(row % 8 == column % 8, dot_nt(rows, spread), 0.0).astype(BF16)

    for xg in range(4):
        cols = []
        for z2 in range(2):
            rows = field[0, :, z2, xg * 16 : (xg + 1) * 16, :].astype(F32)
            cols.append(rows.reshape(32, 2, 8, 128))
        halves = []
        for half in range(2):
            block = jnp.concatenate([c[:, half].reshape(256, 128) for c in cols], axis=1)
            halves.append(dot(left_c[...], block.astype(BF16)))
        for z2 in range(2):
            parts = [h[:, z2 * 128 : (z2 + 1) * 128].reshape(32, 1, 8, 128) for h in halves]
            both = jnp.concatenate(parts, axis=1).reshape(32, 16, 128)
            out[0, :, z2, xg * 16 : (xg + 1) * 16, :] = both.astype(BF16)


def local_mix(field, weight):
    plane = pl.BlockSpec((1, 32, 2, 64, 128), lambda i: (0, 0, i, 0, 0))
    return call(
        local_kernel,
        4,
        [plane, whole((32, 32))],
        plane,
        jax.ShapeDtypeStruct(field.shape, BF16),
        [pltpu.VMEM((256, 256), BF16)],
        1 << 31,
        "local_mix",
        60,
    )(field, weight)


def spread_kernel(weight, order, order_t, out):
    rows = []
    for b2 in range(2):
        for a2 in range(2):
            r = b2 * 2 + a2
            flat = weight[a2, b2].reshape(256, 32).astype(BF16)
            rows.append(dot(flat, order[r * 32 : (r + 1) * 32, :]).astype(BF16))
    for k in range(8):
        block = jnp.concatenate([v[k * 32 : (k + 1) * 32] for v in rows], axis=0)
        out[k] = dot(order_t[...], block).astype(BF16)


def spread_weights(weight, order, order_t):
    return call(
        spread_kernel,
        4,
        [pl.BlockSpec((2, 2, 8, 32, 32), lambda i: (0, 0, i, 0, 0)), whole((128, 128)), whole((128, 128))],
        pl.BlockSpec((8, 128, 128), lambda i: (i, 0, 0)),
        jax.ShapeDtypeStruct((32, 128, 128), BF16),
        [],
        1 << 28,
        "spread_weights",
        16,
    )(weight, order, order_t)


def z_modes(received, left_z, spectrum):
    low_half = lax.broadcasted_iota(jnp.int32, (32, 128), 1) < 64
    for pair in range(8):
        both = [received[s * 128 : (s + 1) * 128, :] for s in (2 * pair, 2 * pair + 1)]
        product = dot(left_z, jnp.concatenate(both, axis=1))
        for odd in range(2):
            p = product[:, odd * 128 : (odd + 1) * 128]
            stay = jnp.where(low_half, p[0:32], p[96:128])
            move = jnp.where(low_half, p[64:96], p[32:64])
            spectrum[pl.ds(2 * pair + odd, 32, stride=16), :] = stay + pltpu.roll(move, 64, axis=1)


def mix_kernel(received, weights, left_z, right_z, out, kept, spectrum, mixed):
    z_modes(received, left_z[...], spectrum)
    kept[...] = spectrum[...].astype(BF16)
    for k in range(32):
        rows = slice(k * 16, (k + 1) * 16)
        mixed[rows, :] = dot(spectrum[rows, :].astype(BF16), weights[k])
    low_half = lax.broadcasted_iota(jnp.int32, (32, 128), 1) < 64
    for pair in range(8):
        blocks = []
        for s in (2 * pair, 2 * pair + 1):
            y = mixed[pl.ds(s, 32, stride=16), :]
            turned = pltpu.roll(y, 64, axis=1)
            stack = [
                jnp.where(low_half, y, 0.0),
                jnp.where(low_half, 0.0, turned),
                jnp.where(low_half, turned, 0.0),
                jnp.where(low_half, 0.0, y),
            ]
            blocks.append(jnp.concatenate(stack, axis=0).astype(BF16))
        product = dot(right_z[...], jnp.concatenate(blocks, axis=1)).astype(BF16)
        for odd in range(2):
            s = 2 * pair + odd
            out[s * 128 : (s + 1) * 128, :] = product[:, odd * 128 : (odd + 1) * 128]


def mix(received, weights, left_z, right_z):
    return call(
        mix_kernel,
        1,
        [whole((2048, 128)), whole((32, 128, 128)), whole((128, 128)), whole((128, 128))],
        [whole((2048, 128)), whole((512, 128))],
        [jax.ShapeDtypeStruct((2048, 128), BF16), jax.ShapeDtypeStruct((512, 128), BF16)],
        [pltpu.VMEM((512, 128), F32), pltpu.VMEM((512, 128), F32)],
        1 << 34,
        "mix_modes",
        16,
    )(received, weights, left_z, right_z)


def gelu_pull(v, cot):
    k = 0.7978845608028654
    square = v * v
    t = jnp.tanh(v * (square * low(k * 0.044715) + low(k)))
    slope = v * (square * low(3.0 * k * 0.044715) + low(k))
    one = low(1.0)
    return cot * ((one + t) * (one + (one - t) * slope))


def low(value):
    return jnp.asarray(value, BF16)


def middle_kernel(received, local, cot, half_x, right_x, left_y, right_y, out, coefficients, planar):
    for pair in range(8):
        both = received[:, pair].astype(F32).reshape(16, 2, 8, 128)
        tiles = [both[:, odd].reshape(128, 128).T.reshape(2, 8, 8, 128) for odd in range(2)]
        coefficients[:, :, pair] = jnp.concatenate(tiles, axis=2).astype(BF16)

    def some(step, carry):
        spectral = []
        for i in range(2):
            halves = [coefficients[z2, step * 2 + i].reshape(128, 128) for z2 in range(2)]
            spectral.append(dot(right_x[...], jnp.concatenate(halves, axis=1)).astype(BF16))
        spectral = jnp.concatenate(spectral, axis=0)
        channels = pl.ds(step * 8, 8)
        planes = []
        for z2 in range(2):
            pre = dot(spectral[:, z2 * 128 : (z2 + 1) * 128], left_y[...]).astype(BF16)
            for zq in range(4):
                z = zq * 2 + z2
                v = pre[:, zq * 128 : (zq + 1) * 128] + local[0, channels, z].reshape(512, 128)
                planes.append(gelu_pull(v, cot[0, channels, z].reshape(512, 128)))
        store_modes(planar, right_y[...], half_x[...], step * 2, planes)
        return carry

    lax.fori_loop(0, 4, some, 0)
    store_messages(planar, out)


def middle(received, local, cot, half_x, right_x, left_y, right_y):
    return call(
        middle_kernel,
        1,
        [
            whole(MESSAGES),
            resident(),
            resident(),
            whole((128, 256)),
            whole((256, 128)),
            whole((128, 512)),
            whole((512, 128)),
        ],
        whole(MESSAGES),
        jax.ShapeDtypeStruct(MESSAGES, BF16),
        [pltpu.VMEM((2, 8, 8, 16, 128), BF16), pltpu.VMEM(PLANAR, F32)],
        1 << 32,
        "gelu_gradient",
        32,
    )(received.reshape(MESSAGES), local, cot, half_x, right_x, left_y, right_y).reshape(2048, 128)


STEP = 8


def update_kernel(
    received, kept, left_z, order_t, weight, moment, second, new_weight, new_moment, new_second, spectrum, results, sems
):
    z_modes(received, left_z[...], spectrum)

    def copies(step):
        some = pl.ds(step * STEP, STEP)
        return [
            pltpu.make_async_copy(results.at[i, :, :, some], target.at[:, :, some], sems.at[i, step])
            for i, target in enumerate((new_weight, new_moment, new_second))
        ]

    for step in range(32 // STEP):
        rows = slice(step * STEP * 16, (step + 1) * STEP * 16)
        left = dot(kept[rows, :], order_t[...]).T.astype(BF16)
        right = dot(spectrum[rows, :].astype(BF16), order_t[...]).astype(BF16)
        zero = jnp.zeros((16, 128), BF16)
        columns = []
        for i in range(STEP):
            tiles = [zero] * STEP
            tiles[i] = right[i * 16 : (i + 1) * 16]
            columns.append(jnp.concatenate(tiles, axis=0))
        product = dot(left, jnp.concatenate(columns, axis=1))
        for i in range(STEP):
            k = step * STEP + i
            for b2 in range(2):
                for a2 in range(2):
                    r = b2 * 2 + a2
                    block = product[r * 32 : (r + 1) * 32, i * 128 : (i + 1) * 128]
                    if r:
                        block = pltpu.roll(block, 128 - 32 * r, axis=1)
                    grad = block[:, :32]
                    w = weight[a2, b2, k]
                    first = beta_one * moment[a2, b2, k] + (1.0 - beta_one) * grad
                    square = beta_two * second[a2, b2, k] + (1.0 - beta_two) * grad * grad
                    first_hat = first / (1.0 - beta_one**adam_step)
                    second_hat = square / (1.0 - beta_two**adam_step)
                    results[1, a2, b2, k] = first
                    results[2, a2, b2, k] = square
                    results[0, a2, b2, k] = w - learn_rate * (
                        first_hat / (jnp.sqrt(second_hat) + adam_eps) + decay_rate * w
                    )
        for copy in copies(step):
            copy.start()
    for step in range(32 // STEP):
        for copy in copies(step):
            copy.wait()


def update(received, kept, left_z, order_t, weight, moment, second):
    return call(
        update_kernel,
        1,
        [whole((2048, 128)), whole((512, 128)), whole((128, 128)), whole((128, 128))] + [resident()] * 3,
        [outside()] * 3,
        [jax.ShapeDtypeStruct(weight.shape, F32)] * 3,
        [
            pltpu.VMEM((512, 128), F32),
            pltpu.VMEM((3,) + weight.shape, F32),
            pltpu.SemaphoreType.DMA((3, 32 // STEP)),
        ],
        1 << 28,
        "adam_update",
        24,
    )(received, kept, left_z, order_t, weight, moment, second)


def exchange(messages):
    return lax.all_to_all(messages, ("dp", "mp"), split_axis=0, concat_axis=0, tiled=True)


def body(field, cotangent, spectral_weight, first_moment, second_moment, local_weight):
    left_x, right_x, half_x, right_y, left_y, left_z, right_z, order, order_t = constants()
    received = exchange(forward(field, left_x, right_y))
    local = local_mix(field, local_weight)
    spread = spread_weights(spectral_weight, order, order_t)
    received, local, spread = lax.optimization_barrier((received, local, spread))
    mixed, kept = mix(received, spread, left_z, right_z)
    received = exchange(mixed)
    received = exchange(middle(received, local, cotangent, half_x, right_x, left_y, right_y))
    return tuple(update(received, kept, left_z, order_t, spectral_weight, first_moment, second_moment))


def solution(mesh):
    spread = P("dp", None, "mp", None, None)
    modes = P("mp", "dp", None, None, None)
    return jax.shard_map(
        body,
        mesh=mesh,
        in_specs=(spread, spread, modes, modes, modes, P()),
        out_specs=(modes, modes, modes),
        check_vma=False,
    )
```

```python
import jax
import jax.numpy as jnp
import ml_dtypes
import numpy as np
from jax import lax
from jax.experimental import pallas as pl
from jax.experimental.pallas import tpu as pltpu
from jax.sharding import PartitionSpec as P

beta_one = 0.9
beta_two = 0.999
learn_rate = 0.001
decay_rate = 0.1
adam_eps = 1e-08
adam_step = 1000.0

F32 = jnp.float32
BF16 = jnp.bfloat16
MIB = 1024 * 1024


def table(length, modes=16):
    grid = np.arange(length, dtype=np.float32)[:, None]
    index = np.arange(2 * modes, dtype=np.float32)[None, :]
    freq = np.where(index < modes, index, index - np.float32(modes - 1)).astype(np.float32)
    phase = (np.float32(2.0 * np.pi) * freq * grid / np.float32(length)).astype(np.float32)
    values = np.where(index < modes, np.cos(phase), np.sin(phase)) * np.sqrt(np.float32(2.0 / length))
    return values.astype(np.float32).astype(ml_dtypes.bfloat16).astype(np.float32)


def constants():
    bx, by, bz = table(64), table(128), table(128)
    left_x = np.einsum("xa,cd->acdx", bx, np.eye(4)).reshape(128, 256)
    right_y = np.einsum("yb,qr->qybr", by, np.eye(4)).reshape(512, 128)
    left_z = np.einsum("nqtk,bd->btkndq", bz.reshape(16, 4, 2, 32), np.eye(2)).reshape(128, 128)
    order = np.eye(128).reshape(2, 2, 8, 4, 128).transpose(0, 2, 1, 3, 4).reshape(128, 128).T
    low = lambda v: jnp.asarray(np.ascontiguousarray(v).astype(ml_dtypes.bfloat16))
    tables = (left_x, left_x.T, left_x * 0.5, right_y, right_y.T, left_z, left_z.T, order, order.T)
    return [low(v) for v in tables]


def dot(a, b):
    return lax.dot_general(a, b, (((1,), (0,)), ((), ())), preferred_element_type=F32)


def dot_nt(a, b):
    return lax.dot_general(a, b, (((1,), (1,)), ((), ())), preferred_element_type=F32)


def whole(shape):
    zeros = (0,) * len(shape)
    return pl.BlockSpec(shape, lambda i: zeros)


def resident():
    return pl.BlockSpec(memory_space=pltpu.VMEM)


def outside():
    return pl.BlockSpec(memory_space=pl.ANY)


def call(kernel, grid, in_specs, out_specs, out_shape, scratch, flops, name, vmem):
    return pl.pallas_call(
        kernel,
        grid=(grid,),
        in_specs=in_specs,
        out_specs=out_specs,
        out_shape=out_shape,
        scratch_shapes=scratch,
        compiler_params=pltpu.CompilerParams(vmem_limit_bytes=vmem * MIB),
        cost_estimate=pl.CostEstimate(flops=flops, bytes_accessed=8 << 20, transcendentals=0),
        name=name,
    )


def y_modes(right_y, planes):
    zero = jnp.zeros((512, 128), BF16)
    both = jnp.concatenate(
        [jnp.concatenate([right_y, zero], axis=1), jnp.concatenate([zero, right_y], axis=1)], axis=0
    )
    return dot(jnp.concatenate(planes, axis=1), both).astype(BF16)


def store_modes(planar, modes, left_x, start):
    for i in range(2):
        product = dot(left_x, modes[i * 256 : (i + 1) * 256, :]).reshape(16, 8, 256)
        for z2 in range(2):
            planar[:, z2, start + i] = product[:, :, z2 * 128 : (z2 + 1) * 128]


def store_messages(planar, out):
    for pair in range(8):
        tiles = [planar[ap].reshape(128, 128).T.reshape(16, 8, 128) for ap in (pair * 2, pair * 2 + 1)]
        out[:, pair] = jnp.concatenate(tiles, axis=1).astype(BF16)


def forward_kernel(field, left_x, left_y, out, first):
    zq = pl.program_id(0)
    for group in range(4):
        halves = []
        for half in range(2):
            rows = slice(group * 8 + half * 4, group * 8 + half * 4 + 4)
            block = jnp.concatenate([field[0, rows, z2].reshape(256, 128) for z2 in range(2)], axis=1)
            halves.append(dot(left_x[...], block).reshape(16, 1, 8, 256))
        both = jnp.concatenate(halves, axis=1).reshape(16, 16, 256).astype(BF16)
        for z2 in range(2):
            first[:, zq, z2, group] = both[:, :, z2 * 128 : (z2 + 1) * 128]

    @pl.when(zq == 3)
    def _():
        for pair in range(8):
            planes = [first[pair * 2 : pair * 2 + 2, q].reshape(256, 128) for q in range(4)]
            planar = dot_nt(left_y[...], jnp.concatenate(planes, axis=1))
            tiles = [planar[:, :128].reshape(16, 8, 128), planar[:, 128:].reshape(16, 8, 128)]
            out[:, pair] = jnp.concatenate(tiles, axis=1).astype(BF16)


PLANAR = (16, 2, 8, 8, 128)
MESSAGES = (16, 8, 16, 128)


def forward(field, left_x, left_y):
    return call(
        forward_kernel,
        4,
        [
            pl.BlockSpec((1, 32, 2, 64, 128), lambda i: (0, 0, i, 0, 0)),
            whole((128, 256)),
            whole((128, 512)),
        ],
        whole(MESSAGES),
        jax.ShapeDtypeStruct(MESSAGES, BF16),
        [pltpu.VMEM((16, 4, 2, 4, 16, 128), BF16)],
        1 << 31,
        "planes_to_modes",
        60,
    )(field, left_x, left_y).reshape(2048, 128)


def local_kernel(field, weight, out, left_c):
    @pl.when(pl.program_id(0) == 0)
    def _():
        row = lax.broadcasted_iota(jnp.int32, (256, 32), 0)
        column = lax.broadcasted_iota(jnp.int32, (256, 32), 1)
        spread = jnp.where(row // 8 == column, 1.0, 0.0).astype(BF16)
        rows = dot_nt(spread, weight[...]).astype(BF16)
        row = lax.broadcasted_iota(jnp.int32, (256, 256), 0)
        column = lax.broadcasted_iota(jnp.int32, (256, 256), 1)
        left_c[...] = jnp.where(row % 8 == column % 8, dot_nt(rows, spread), 0.0).astype(BF16)

    for xg in range(4):
        cols = []
        for z2 in range(2):
            rows = field[0, :, z2, xg * 16 : (xg + 1) * 16, :].astype(F32)
            cols.append(rows.reshape(32, 2, 8, 128))
        halves = []
        for half in range(2):
            block = jnp.concatenate([c[:, half].reshape(256, 128) for c in cols], axis=1)
            halves.append(dot(left_c[...], block.astype(BF16)))
        for z2 in range(2):
            parts = [h[:, z2 * 128 : (z2 + 1) * 128].reshape(32, 1, 8, 128) for h in halves]
            both = jnp.concatenate(parts, axis=1).reshape(32, 16, 128)
            out[0, :, z2, xg * 16 : (xg + 1) * 16, :] = both.astype(BF16)


def local_mix(field, weight):
    plane = pl.BlockSpec((1, 32, 2, 64, 128), lambda i: (0, 0, i, 0, 0))
    return call(
        local_kernel,
        4,
        [plane, whole((32, 32))],
        plane,
        jax.ShapeDtypeStruct(field.shape, BF16),
        [pltpu.VMEM((256, 256), BF16)],
        1 << 31,
        "local_mix",
        60,
    )(field, weight)


def spread_kernel(weight, order, order_t, out):
    rows = []
    for b2 in range(2):
        for a2 in range(2):
            r = b2 * 2 + a2
            flat = weight[a2, b2].reshape(256, 32).astype(BF16)
            rows.append(dot(flat, order[r * 32 : (r + 1) * 32, :]).astype(BF16))
    for k in range(8):
        block = jnp.concatenate([v[k * 32 : (k + 1) * 32] for v in rows], axis=0)
        out[k] = dot(order_t[...], block).astype(BF16)


def spread_weights(weight, order, order_t):
    return call(
        spread_kernel,
        4,
        [pl.BlockSpec((2, 2, 8, 32, 32), lambda i: (0, 0, i, 0, 0)), whole((128, 128)), whole((128, 128))],
        pl.BlockSpec((8, 128, 128), lambda i: (i, 0, 0)),
        jax.ShapeDtypeStruct((32, 128, 128), BF16),
        [],
        1 << 28,
        "spread_weights",
        16,
    )(weight, order, order_t)


def z_modes(received, left_z, spectrum):
    low_half = lax.broadcasted_iota(jnp.int32, (32, 128), 1) < 64
    for pair in range(8):
        both = [received[s * 128 : (s + 1) * 128, :] for s in (2 * pair, 2 * pair + 1)]
        product = dot(left_z, jnp.concatenate(both, axis=1))
        for odd in range(2):
            p = product[:, odd * 128 : (odd + 1) * 128]
            stay = jnp.where(low_half, p[0:32], p[96:128])
            move = jnp.where(low_half, p[64:96], p[32:64])
            spectrum[pl.ds(2 * pair + odd, 32, stride=16), :] = stay + pltpu.roll(move, 64, axis=1)


def mix_kernel(received, weights, left_z, right_z, out, kept, spectrum, mixed):
    z_modes(received, left_z[...], spectrum)
    kept[...] = spectrum[...].astype(BF16)
    for k in range(32):
        rows = slice(k * 16, (k + 1) * 16)
        mixed[rows, :] = dot(spectrum[rows, :].astype(BF16), weights[k])
    low_half = lax.broadcasted_iota(jnp.int32, (32, 128), 1) < 64
    for pair in range(8):
        blocks = []
        for s in (2 * pair, 2 * pair + 1):
            y = mixed[pl.ds(s, 32, stride=16), :]
            turned = pltpu.roll(y, 64, axis=1)
            stack = [
                jnp.where(low_half, y, 0.0),
                jnp.where(low_half, 0.0, turned),
                jnp.where(low_half, turned, 0.0),
                jnp.where(low_half, 0.0, y),
            ]
            blocks.append(jnp.concatenate(stack, axis=0).astype(BF16))
        product = dot(right_z[...], jnp.concatenate(blocks, axis=1)).astype(BF16)
        for odd in range(2):
            s = 2 * pair + odd
            out[s * 128 : (s + 1) * 128, :] = product[:, odd * 128 : (odd + 1) * 128]


def mix(received, weights, left_z, right_z):
    return call(
        mix_kernel,
        1,
        [whole((2048, 128)), whole((32, 128, 128)), whole((128, 128)), whole((128, 128))],
        [whole((2048, 128)), whole((512, 128))],
        [jax.ShapeDtypeStruct((2048, 128), BF16), jax.ShapeDtypeStruct((512, 128), BF16)],
        [pltpu.VMEM((512, 128), F32), pltpu.VMEM((512, 128), F32)],
        1 << 34,
        "mix_modes",
        16,
    )(received, weights, left_z, right_z)


def gelu_pull(v, cot):
    k = 0.7978845608028654
    square = v * v
    t = jnp.tanh(v * (square * low(k * 0.044715) + low(k)))
    slope = v * (square * low(3.0 * k * 0.044715) + low(k))
    one = low(1.0)
    return (one + t) * (one + (one - t) * slope) * cot


def low(value):
    return jnp.asarray(value, BF16)


def middle_kernel(
    received, local, cot, half_x, right_x, left_y, right_y, out, coefficients, planar, spectral, modes
):
    for pair in range(8):
        both = received[:, pair].astype(F32).reshape(16, 2, 8, 128)
        tiles = [both[:, odd].reshape(128, 128).T.reshape(2, 8, 8, 128) for odd in range(2)]
        coefficients[:, :, pair] = jnp.concatenate(tiles, axis=2).astype(BF16)

    def inverse_x(step):
        for i in range(2):
            halves = [coefficients[z2, step * 2 + i].reshape(128, 128) for z2 in range(2)]
            rows = slice(i * 256, (i + 1) * 256)
            spectral[rows, :] = dot(right_x[...], jnp.concatenate(halves, axis=1)).astype(BF16)

    def some(step, carry):
        store_modes(planar, modes, half_x[...], jnp.maximum(step - 1, 0) * 2)
        channels = pl.ds(step * 8, 8)
        planes = []
        for z2 in range(2):
            pre = dot(spectral[:, z2 * 128 : (z2 + 1) * 128], left_y[...]).astype(BF16)
            for zq in range(4):
                z = zq * 2 + z2
                v = pre[:, zq * 128 : (zq + 1) * 128] + local[0, channels, z].reshape(512, 128)
                planes.append(gelu_pull(v, cot[0, channels, z].reshape(512, 128)))
        inverse_x(jnp.minimum(step + 1, 3))
        modes[...] = y_modes(right_y[...], planes)
        return carry

    inverse_x(0)
    modes[...] = jnp.zeros((512, 256), BF16)
    lax.fori_loop(0, 4, some, 0)
    store_modes(planar, modes, half_x[...], 6)
    store_messages(planar, out)


def middle(received, local, cot, half_x, right_x, left_y, right_y):
    return call(
        middle_kernel,
        1,
        [
            whole(MESSAGES),
            resident(),
            resident(),
            whole((128, 256)),
            whole((256, 128)),
            whole((128, 512)),
            whole((512, 128)),
        ],
        whole(MESSAGES),
        jax.ShapeDtypeStruct(MESSAGES, BF16),
        [
            pltpu.VMEM((2, 8, 8, 16, 128), BF16),
            pltpu.VMEM(PLANAR, F32),
            pltpu.VMEM((512, 256), BF16),
            pltpu.VMEM((512, 256), BF16),
        ],
        1 << 32,
        "gelu_gradient",
        32,
    )(received.reshape(MESSAGES), local, cot, half_x, right_x, left_y, right_y).reshape(2048, 128)


STEP = 8


def update_kernel(
    received, kept, left_z, order_t, weight, moment, second, new_weight, new_moment, new_second, spectrum, results, sems
):
    z_modes(received, left_z[...], spectrum)

    def copies(step):
        some = pl.ds(step * STEP, STEP)
        return [
            pltpu.make_async_copy(results.at[i, :, :, some], target.at[:, :, some], sems.at[i, step])
            for i, target in enumerate((new_weight, new_moment, new_second))
        ]

    for step in range(32 // STEP):
        rows = slice(step * STEP * 16, (step + 1) * STEP * 16)
        left = dot(kept[rows, :], order_t[...]).T.astype(BF16)
        right = dot(spectrum[rows, :].astype(BF16), order_t[...]).astype(BF16)
        zero = jnp.zeros((16, 128), BF16)
        columns = []
        for i in range(STEP):
            tiles = [zero] * STEP
            tiles[i] = right[i * 16 : (i + 1) * 16]
            columns.append(jnp.concatenate(tiles, axis=0))
        product = dot(left, jnp.concatenate(columns, axis=1))
        for i in range(STEP):
            k = step * STEP + i
            for b2 in range(2):
                for a2 in range(2):
                    r = b2 * 2 + a2
                    block = product[r * 32 : (r + 1) * 32, i * 128 : (i + 1) * 128]
                    if r:
                        block = pltpu.roll(block, 128 - 32 * r, axis=1)
                    grad = block[:, :32]
                    w = weight[a2, b2, k]
                    first = beta_one * moment[a2, b2, k] + (1.0 - beta_one) * grad
                    square = beta_two * second[a2, b2, k] + (1.0 - beta_two) * grad * grad
                    first_hat = first / (1.0 - beta_one**adam_step)
                    second_hat = square / (1.0 - beta_two**adam_step)
                    results[1, a2, b2, k] = first
                    results[2, a2, b2, k] = square
                    results[0, a2, b2, k] = w - learn_rate * (
                        first_hat / (jnp.sqrt(second_hat) + adam_eps) + decay_rate * w
                    )
        for copy in copies(step):
            copy.start()
    for step in range(32 // STEP):
        for copy in copies(step):
            copy.wait()


def update(received, kept, left_z, order_t, weight, moment, second):
    return call(
        update_kernel,
        1,
        [whole((2048, 128)), whole((512, 128)), whole((128, 128)), whole((128, 128))] + [resident()] * 3,
        [outside()] * 3,
        [jax.ShapeDtypeStruct(weight.shape, F32)] * 3,
        [
            pltpu.VMEM((512, 128), F32),
            pltpu.VMEM((3,) + weight.shape, F32),
            pltpu.SemaphoreType.DMA((3, 32 // STEP)),
        ],
        1 << 28,
        "adam_update",
        24,
    )(received, kept, left_z, order_t, weight, moment, second)


def exchange(messages):
    return lax.all_to_all(messages, ("dp", "mp"), split_axis=0, concat_axis=0, tiled=True)


def body(field, cotangent, spectral_weight, first_moment, second_moment, local_weight):
    left_x, right_x, half_x, right_y, left_y, left_z, right_z, order, order_t = constants()
    received = exchange(forward(field, left_x, left_y))
    local = local_mix(field, local_weight)
    spread = spread_weights(spectral_weight, order, order_t)
    received, local, spread = lax.optimization_barrier((received, local, spread))
    mixed, kept = mix(received, spread, left_z, right_z)
    received = exchange(mixed)
    received = exchange(middle(received, local, cotangent, half_x, right_x, left_y, right_y))
    return tuple(update(received, kept, left_z, order_t, spectral_weight, first_moment, second_moment))


def solution(mesh):
    spread = P("dp", None, "mp", None, None)
    modes = P("mp", "dp", None, None, None)
    return jax.shard_map(
        body,
        mesh=mesh,
        in_specs=(spread, spread, modes, modes, modes, P()),
        out_specs=(modes, modes, modes),
        check_vma=False,
    )
```

```python
import jax
import jax.numpy as jnp
import ml_dtypes
import numpy as np
from jax import lax
from jax.experimental import pallas as pl
from jax.experimental.pallas import tpu as pltpu
from jax.sharding import PartitionSpec as P

beta_one = 0.9
beta_two = 0.999
learn_rate = 0.001
decay_rate = 0.1
adam_eps = 1e-08
adam_step = 1000.0

F32 = jnp.float32
BF16 = jnp.bfloat16
MIB = 1024 * 1024


def table(length, modes=16):
    grid = np.arange(length, dtype=np.float32)[:, None]
    index = np.arange(2 * modes, dtype=np.float32)[None, :]
    freq = np.where(index < modes, index, index - np.float32(modes - 1)).astype(np.float32)
    phase = (np.float32(2.0 * np.pi) * freq * grid / np.float32(length)).astype(np.float32)
    values = np.where(index < modes, np.cos(phase), np.sin(phase)) * np.sqrt(np.float32(2.0 / length))
    return values.astype(np.float32).astype(ml_dtypes.bfloat16).astype(np.float32)


def constants():
    bx, by, bz = table(64), table(128), table(128)
    left_x = np.einsum("xa,cd->acdx", bx, np.eye(4)).reshape(128, 256)
    right_y = np.einsum("yb,qr->qybr", by, np.eye(4)).reshape(512, 128)
    left_z = np.einsum("nqtk,bd->btkndq", bz.reshape(16, 4, 2, 32), np.eye(2)).reshape(128, 128)
    order = np.eye(128).reshape(2, 2, 8, 4, 128).transpose(0, 2, 1, 3, 4).reshape(128, 128).T
    low = lambda v: jnp.asarray(np.ascontiguousarray(v).astype(ml_dtypes.bfloat16))
    tables = (left_x, left_x.T, left_x * 0.5, right_y, right_y.T, left_z, left_z.T, order, order.T)
    return [low(v) for v in tables]


def dot(a, b):
    return lax.dot_general(a, b, (((1,), (0,)), ((), ())), preferred_element_type=F32)


def dot_nt(a, b):
    return lax.dot_general(a, b, (((1,), (1,)), ((), ())), preferred_element_type=F32)


def whole(shape):
    zeros = (0,) * len(shape)
    return pl.BlockSpec(shape, lambda i: zeros)


def resident():
    return pl.BlockSpec(memory_space=pltpu.VMEM)


def outside():
    return pl.BlockSpec(memory_space=pl.ANY)


def call(kernel, grid, in_specs, out_specs, out_shape, scratch, flops, name, vmem):
    return pl.pallas_call(
        kernel,
        grid=(grid,),
        in_specs=in_specs,
        out_specs=out_specs,
        out_shape=out_shape,
        scratch_shapes=scratch,
        compiler_params=pltpu.CompilerParams(vmem_limit_bytes=vmem * MIB),
        cost_estimate=pl.CostEstimate(flops=flops, bytes_accessed=8 << 20, transcendentals=0),
        name=name,
    )


def y_modes(right_y, planes):
    zero = jnp.zeros((512, 128), BF16)
    both = jnp.concatenate(
        [jnp.concatenate([right_y, zero], axis=1), jnp.concatenate([zero, right_y], axis=1)], axis=0
    )
    return dot(jnp.concatenate(planes, axis=1), both).astype(BF16)


def store_modes(planar, modes, left_x, start):
    for i in range(2):
        product = dot(left_x, modes[i * 256 : (i + 1) * 256, :]).reshape(16, 8, 256)
        for z2 in range(2):
            planar[:, z2, start + i] = product[:, :, z2 * 128 : (z2 + 1) * 128]


def store_messages(planar, out):
    for pair in range(8):
        tiles = [planar[ap].reshape(128, 128).T.reshape(16, 8, 128) for ap in (pair * 2, pair * 2 + 1)]
        out[:, pair] = jnp.concatenate(tiles, axis=1).astype(BF16)


def forward_kernel(field, left_x, right_y, out, buffer, left_buffer, right_buffer, planar, sems, table_sems):
    def copy(part):
        rows = pl.ds(part * 8, 8)
        return pltpu.make_async_copy(field.at[0, rows], buffer.at[rows], sems.at[part])

    tables = [
        pltpu.make_async_copy(right_y, right_buffer, table_sems.at[0]),
        pltpu.make_async_copy(left_x, left_buffer, table_sems.at[1]),
    ]
    copy(0).start()
    for table_copy in tables:
        table_copy.start()
    copy(1).start()
    for table_copy in tables:
        table_copy.wait()

    def some(step, carry):
        copy(step).wait()

        @pl.when(step < 2)
        def _():
            copy(step + 2).start()

        block = buffer[pl.ds(step * 8, 8)]
        planes = [block[:, zq * 2 + z2].reshape(512, 128) for z2 in range(2) for zq in range(4)]
        store_modes(planar, y_modes(right_buffer[...], planes), left_buffer[...], step * 2)
        return carry

    lax.fori_loop(0, 4, some, 0)
    store_messages(planar, out)


PLANAR = (16, 2, 8, 8, 128)
MESSAGES = (16, 8, 16, 128)


def forward(field, left_x, right_y):
    return call(
        forward_kernel,
        1,
        [outside()] * 3,
        whole(MESSAGES),
        jax.ShapeDtypeStruct(MESSAGES, BF16),
        [
            pltpu.VMEM((32, 8, 64, 128), BF16),
            pltpu.VMEM((128, 256), BF16),
            pltpu.VMEM((512, 128), BF16),
            pltpu.VMEM(PLANAR, F32),
            pltpu.SemaphoreType.DMA((4,)),
            pltpu.SemaphoreType.DMA((2,)),
        ],
        1 << 31,
        "planes_to_modes",
        60,
    )(field, left_x, right_y).reshape(2048, 128)


def local_kernel(field, weight, out, left_c):
    @pl.when(pl.program_id(0) == 0)
    def _():
        row = lax.broadcasted_iota(jnp.int32, (256, 32), 0)
        column = lax.broadcasted_iota(jnp.int32, (256, 32), 1)
        spread = jnp.where(row // 8 == column, 1.0, 0.0).astype(BF16)
        rows = dot_nt(spread, weight[...]).astype(BF16)
        row = lax.broadcasted_iota(jnp.int32, (256, 256), 0)
        column = lax.broadcasted_iota(jnp.int32, (256, 256), 1)
        left_c[...] = jnp.where(row % 8 == column % 8, dot_nt(rows, spread), 0.0).astype(BF16)

    for xg in range(4):
        cols = []
        for z2 in range(2):
            rows = field[0, :, z2, xg * 16 : (xg + 1) * 16, :].astype(F32)
            cols.append(rows.reshape(32, 2, 8, 128))
        halves = []
        for half in range(2):
            block = jnp.concatenate([c[:, half].reshape(256, 128) for c in cols], axis=1)
            halves.append(dot(left_c[...], block.astype(BF16)))
        for z2 in range(2):
            parts = [h[:, z2 * 128 : (z2 + 1) * 128].reshape(32, 1, 8, 128) for h in halves]
            both = jnp.concatenate(parts, axis=1).reshape(32, 16, 128)
            out[0, :, z2, xg * 16 : (xg + 1) * 16, :] = both.astype(BF16)


def local_mix(field, weight):
    plane = pl.BlockSpec((1, 32, 2, 64, 128), lambda i: (0, 0, i, 0, 0))
    return call(
        local_kernel,
        4,
        [plane, whole((32, 32))],
        plane,
        jax.ShapeDtypeStruct(field.shape, BF16),
        [pltpu.VMEM((256, 256), BF16)],
        1 << 31,
        "local_mix",
        60,
    )(field, weight)


def spread_kernel(weight, order, order_t, out):
    rows = []
    for b2 in range(2):
        for a2 in range(2):
            r = b2 * 2 + a2
            flat = weight[a2, b2].reshape(256, 32).astype(BF16)
            rows.append(dot(flat, order[r * 32 : (r + 1) * 32, :]).astype(BF16))
    for k in range(8):
        block = jnp.concatenate([v[k * 32 : (k + 1) * 32] for v in rows], axis=0)
        out[k] = dot(order_t[...], block).astype(BF16)


def spread_weights(weight, order, order_t):
    return call(
        spread_kernel,
        4,
        [pl.BlockSpec((2, 2, 8, 32, 32), lambda i: (0, 0, i, 0, 0)), whole((128, 128)), whole((128, 128))],
        pl.BlockSpec((8, 128, 128), lambda i: (i, 0, 0)),
        jax.ShapeDtypeStruct((32, 128, 128), BF16),
        [],
        1 << 28,
        "spread_weights",
        16,
    )(weight, order, order_t)


def z_modes(received, left_z, spectrum):
    low_half = lax.broadcasted_iota(jnp.int32, (32, 128), 1) < 64
    for pair in range(8):
        both = [received[s * 128 : (s + 1) * 128, :] for s in (2 * pair, 2 * pair + 1)]
        product = dot(left_z, jnp.concatenate(both, axis=1))
        for odd in range(2):
            p = product[:, odd * 128 : (odd + 1) * 128]
            stay = jnp.where(low_half, p[0:32], p[96:128])
            move = jnp.where(low_half, p[64:96], p[32:64])
            spectrum[pl.ds(2 * pair + odd, 32, stride=16), :] = stay + pltpu.roll(move, 64, axis=1)


def mix_kernel(received, weights, left_z, right_z, out, kept, spectrum, mixed):
    z_modes(received, left_z[...], spectrum)
    kept[...] = spectrum[...].astype(BF16)
    for k in range(32):
        rows = slice(k * 16, (k + 1) * 16)
        mixed[rows, :] = dot(spectrum[rows, :].astype(BF16), weights[k])
    low_half = lax.broadcasted_iota(jnp.int32, (32, 128), 1) < 64
    for pair in range(8):
        blocks = []
        for s in (2 * pair, 2 * pair + 1):
            y = mixed[pl.ds(s, 32, stride=16), :]
            turned = pltpu.roll(y, 64, axis=1)
            stack = [
                jnp.where(low_half, y, 0.0),
                jnp.where(low_half, 0.0, turned),
                jnp.where(low_half, turned, 0.0),
                jnp.where(low_half, 0.0, y),
            ]
            blocks.append(jnp.concatenate(stack, axis=0).astype(BF16))
        product = dot(right_z[...], jnp.concatenate(blocks, axis=1)).astype(BF16)
        for odd in range(2):
            s = 2 * pair + odd
            out[s * 128 : (s + 1) * 128, :] = product[:, odd * 128 : (odd + 1) * 128]


def mix(received, weights, left_z, right_z):
    return call(
        mix_kernel,
        1,
        [whole((2048, 128)), whole((32, 128, 128)), whole((128, 128)), whole((128, 128))],
        [whole((2048, 128)), whole((512, 128))],
        [jax.ShapeDtypeStruct((2048, 128), BF16), jax.ShapeDtypeStruct((512, 128), BF16)],
        [pltpu.VMEM((512, 128), F32), pltpu.VMEM((512, 128), F32)],
        1 << 34,
        "mix_modes",
        16,
    )(received, weights, left_z, right_z)


def gelu_pull(v, cot):
    k = 0.7978845608028654
    square = v * v
    t = jnp.tanh(v * (square * low(k * 0.044715) + low(k)))
    slope = v * (square * low(3.0 * k * 0.044715) + low(k))
    one = low(1.0)
    return (one + t) * (one + (one - t) * slope) * cot


def low(value):
    return jnp.asarray(value, BF16)


def middle_kernel(
    received, local, cot, half_x, right_x, left_y, right_y, out, coefficients, planar, spectral, modes
):
    for pair in range(8):
        both = received[:, pair].astype(F32).reshape(16, 2, 8, 128)
        tiles = [both[:, odd].reshape(128, 128).T.reshape(2, 8, 8, 128) for odd in range(2)]
        coefficients[:, :, pair] = jnp.concatenate(tiles, axis=2).astype(BF16)

    def inverse_x(step):
        for i in range(2):
            halves = [coefficients[z2, step * 2 + i].reshape(128, 128) for z2 in range(2)]
            rows = slice(i * 256, (i + 1) * 256)
            spectral[rows, :] = dot(right_x[...], jnp.concatenate(halves, axis=1)).astype(BF16)

    def some(step, carry):
        store_modes(planar, modes, half_x[...], jnp.maximum(step - 1, 0) * 2)
        channels = pl.ds(step * 8, 8)
        planes = []
        for z2 in range(2):
            pre = dot(spectral[:, z2 * 128 : (z2 + 1) * 128], left_y[...]).astype(BF16)
            for zq in range(4):
                z = zq * 2 + z2
                v = pre[:, zq * 128 : (zq + 1) * 128] + local[0, channels, z].reshape(512, 128)
                planes.append(gelu_pull(v, cot[0, channels, z].reshape(512, 128)))
        inverse_x(jnp.minimum(step + 1, 3))
        modes[...] = y_modes(right_y[...], planes)
        return carry

    inverse_x(0)
    modes[...] = jnp.zeros((512, 256), BF16)
    lax.fori_loop(0, 4, some, 0)
    store_modes(planar, modes, half_x[...], 6)
    store_messages(planar, out)


def middle(received, local, cot, half_x, right_x, left_y, right_y):
    return call(
        middle_kernel,
        1,
        [
            whole(MESSAGES),
            resident(),
            resident(),
            whole((128, 256)),
            whole((256, 128)),
            whole((128, 512)),
            whole((512, 128)),
        ],
        whole(MESSAGES),
        jax.ShapeDtypeStruct(MESSAGES, BF16),
        [
            pltpu.VMEM((2, 8, 8, 16, 128), BF16),
            pltpu.VMEM(PLANAR, F32),
            pltpu.VMEM((512, 256), BF16),
            pltpu.VMEM((512, 256), BF16),
        ],
        1 << 32,
        "gelu_gradient",
        32,
    )(received.reshape(MESSAGES), local, cot, half_x, right_x, left_y, right_y).reshape(2048, 128)


STEP = 16


def update_kernel(
    received, kept, left_z, order_t, weight, moment, second, new_weight, new_moment, new_second, spectrum, results, sems
):
    z_modes(received, left_z[...], spectrum)

    def copies(step):
        some = pl.ds(step * STEP, STEP)
        return [
            pltpu.make_async_copy(results.at[i, :, :, some], target.at[:, :, some], sems.at[i, step])
            for i, target in enumerate((new_weight, new_moment, new_second))
        ]

    for step in range(32 // STEP):
        rows = slice(step * STEP * 16, (step + 1) * STEP * 16)
        left = dot(kept[rows, :], order_t[...]).T.astype(BF16)
        right = dot(spectrum[rows, :].astype(BF16), order_t[...]).astype(BF16)
        zero = jnp.zeros((16, 128), BF16)
        columns = []
        for i in range(STEP):
            tiles = [zero] * STEP
            tiles[i] = right[i * 16 : (i + 1) * 16]
            columns.append(jnp.concatenate(tiles, axis=0))
        product = dot(left, jnp.concatenate(columns, axis=1))
        for i in range(STEP):
            k = step * STEP + i
            for b2 in range(2):
                for a2 in range(2):
                    r = b2 * 2 + a2
                    block = product[r * 32 : (r + 1) * 32, i * 128 : (i + 1) * 128]
                    if r:
                        block = pltpu.roll(block, 128 - 32 * r, axis=1)
                    grad = block[:, :32]
                    first = beta_one * moment[a2, b2, k] + (1.0 - beta_one) * grad
                    square = beta_two * second[a2, b2, k] + (1.0 - beta_two) * grad * grad
                    results[1, a2, b2, k] = first
                    results[2, a2, b2, k] = square
                    second_hat = square * (1.0 / (1.0 - beta_two**adam_step))
                    root = second_hat * lax.rsqrt(second_hat)
                    scaled = first * (learn_rate / (1.0 - beta_one**adam_step))
                    kept_weight = weight[a2, b2, k] * (1.0 - learn_rate * decay_rate)
                    results[0, a2, b2, k] = kept_weight - scaled / (root + adam_eps)
        for copy in copies(step):
            copy.start()
    for step in range(32 // STEP):
        for copy in copies(step):
            copy.wait()


def update(received, kept, left_z, order_t, weight, moment, second):
    return call(
        update_kernel,
        1,
        [whole((2048, 128)), whole((512, 128)), whole((128, 128)), whole((128, 128))] + [resident()] * 3,
        [outside()] * 3,
        [jax.ShapeDtypeStruct(weight.shape, F32)] * 3,
        [
            pltpu.VMEM((512, 128), F32),
            pltpu.VMEM((3,) + weight.shape, F32),
            pltpu.SemaphoreType.DMA((3, 32 // STEP)),
        ],
        1 << 28,
        "adam_update",
        24,
    )(received, kept, left_z, order_t, weight, moment, second)


def exchange(messages):
    return lax.all_to_all(messages, ("dp", "mp"), split_axis=0, concat_axis=0, tiled=True)


def body(field, cotangent, spectral_weight, first_moment, second_moment, local_weight):
    left_x, right_x, half_x, right_y, left_y, left_z, right_z, order, order_t = constants()
    received = exchange(forward(field, left_x, right_y))
    local = local_mix(field, local_weight)
    spread = spread_weights(spectral_weight, order, order_t)
    received, local, spread = lax.optimization_barrier((received, local, spread))
    mixed, kept = mix(received, spread, left_z, right_z)
    received = exchange(mixed)
    received = exchange(middle(received, local, cotangent, half_x, right_x, left_y, right_y))
    return tuple(update(received, kept, left_z, order_t, spectral_weight, first_moment, second_moment))


def solution(mesh):
    spread = P("dp", None, "mp", None, None)
    modes = P("mp", "dp", None, None, None)
    return jax.shard_map(
        body,
        mesh=mesh,
        in_specs=(spread, spread, modes, modes, modes, P()),
        out_specs=(modes, modes, modes),
        check_vma=False,
    )
```

```python
import jax
import jax.numpy as jnp
import ml_dtypes
import numpy as np
from jax import lax
from jax.experimental import pallas as pl
from jax.experimental.pallas import tpu as pltpu
from jax.sharding import PartitionSpec as P

beta_one = 0.9
beta_two = 0.999
learn_rate = 0.001
decay_rate = 0.1
adam_eps = 1e-08
adam_step = 1000.0

F32 = jnp.float32
BF16 = jnp.bfloat16
MIB = 1024 * 1024


def table(length, modes=16):
    grid = np.arange(length, dtype=np.float32)[:, None]
    index = np.arange(2 * modes, dtype=np.float32)[None, :]
    freq = np.where(index < modes, index, index - np.float32(modes - 1)).astype(np.float32)
    phase = (np.float32(2.0 * np.pi) * freq * grid / np.float32(length)).astype(np.float32)
    values = np.where(index < modes, np.cos(phase), np.sin(phase)) * np.sqrt(np.float32(2.0 / length))
    return values.astype(np.float32).astype(ml_dtypes.bfloat16).astype(np.float32)


def constants():
    bx, by, bz = table(64), table(128), table(128)
    left_x = np.einsum("xa,cd->acdx", bx, np.eye(4)).reshape(128, 256)
    right_y = np.einsum("yb,qr->qybr", by, np.eye(4)).reshape(512, 128)
    left_z = np.einsum("nqtk,bd->btkndq", bz.reshape(16, 4, 2, 32), np.eye(2)).reshape(128, 128)
    order = np.eye(128).reshape(2, 2, 8, 4, 128).transpose(0, 2, 1, 3, 4).reshape(128, 128).T
    low = lambda v: jnp.asarray(np.ascontiguousarray(v).astype(ml_dtypes.bfloat16))
    tables = (left_x, left_x.T, left_x * 0.5, right_y, right_y.T, left_z, left_z.T, order, order.T)
    return [low(v) for v in tables]


def dot(a, b):
    return lax.dot_general(a, b, (((1,), (0,)), ((), ())), preferred_element_type=F32)


def dot_nt(a, b):
    return lax.dot_general(a, b, (((1,), (1,)), ((), ())), preferred_element_type=F32)


def whole(shape):
    zeros = (0,) * len(shape)
    return pl.BlockSpec(shape, lambda i: zeros)


def resident():
    return pl.BlockSpec(memory_space=pltpu.VMEM)


def outside():
    return pl.BlockSpec(memory_space=pl.ANY)


def call(kernel, grid, in_specs, out_specs, out_shape, scratch, flops, name, vmem):
    return pl.pallas_call(
        kernel,
        grid=(grid,),
        in_specs=in_specs,
        out_specs=out_specs,
        out_shape=out_shape,
        scratch_shapes=scratch,
        compiler_params=pltpu.CompilerParams(vmem_limit_bytes=vmem * MIB),
        cost_estimate=pl.CostEstimate(flops=flops, bytes_accessed=8 << 20, transcendentals=0),
        name=name,
    )


def y_modes(right_y, planes):
    zero = jnp.zeros((512, 128), BF16)
    both = jnp.concatenate(
        [jnp.concatenate([right_y, zero], axis=1), jnp.concatenate([zero, right_y], axis=1)], axis=0
    )
    return dot(jnp.concatenate(planes, axis=1), both).astype(BF16)


def store_modes(planar, modes, left_x, start):
    for i in range(2):
        product = dot(left_x, modes[i * 256 : (i + 1) * 256, :]).reshape(16, 8, 256)
        for z2 in range(2):
            planar[:, z2, start + i] = product[:, :, z2 * 128 : (z2 + 1) * 128]


def store_messages(planar, out):
    for pair in range(8):
        tiles = [planar[ap].reshape(128, 128).T.reshape(16, 8, 128) for ap in (pair * 2, pair * 2 + 1)]
        out[:, pair] = jnp.concatenate(tiles, axis=1).astype(BF16)


def forward_kernel(field, left_x, right_y, out, buffer, left_buffer, right_buffer, planar, sems, table_sems):
    def copy(part):
        rows = pl.ds(part * 8, 8)
        return pltpu.make_async_copy(field.at[0, rows], buffer.at[rows], sems.at[part])

    tables = [
        pltpu.make_async_copy(right_y, right_buffer, table_sems.at[0]),
        pltpu.make_async_copy(left_x, left_buffer, table_sems.at[1]),
    ]
    copy(0).start()
    for table_copy in tables:
        table_copy.start()
    copy(1).start()
    for table_copy in tables:
        table_copy.wait()

    def some(step, carry):
        copy(step).wait()

        @pl.when(step < 2)
        def _():
            copy(step + 2).start()

        block = buffer[pl.ds(step * 8, 8)]
        planes = [block[:, zq * 2 + z2].reshape(512, 128) for z2 in range(2) for zq in range(4)]
        store_modes(planar, y_modes(right_buffer[...], planes), left_buffer[...], step * 2)
        return carry

    lax.fori_loop(0, 4, some, 0)
    store_messages(planar, out)


PLANAR = (16, 2, 8, 8, 128)
MESSAGES = (16, 8, 16, 128)


def forward(field, left_x, right_y):
    return call(
        forward_kernel,
        1,
        [outside()] * 3,
        whole(MESSAGES),
        jax.ShapeDtypeStruct(MESSAGES, BF16),
        [
            pltpu.VMEM((32, 8, 64, 128), BF16),
            pltpu.VMEM((128, 256), BF16),
            pltpu.VMEM((512, 128), BF16),
            pltpu.VMEM(PLANAR, F32),
            pltpu.SemaphoreType.DMA((4,)),
            pltpu.SemaphoreType.DMA((2,)),
        ],
        1 << 31,
        "planes_to_modes",
        60,
    )(field, left_x, right_y).reshape(2048, 128)


def local_kernel(field, weight, out, left_c):
    @pl.when(pl.program_id(0) == 0)
    def _():
        row = lax.broadcasted_iota(jnp.int32, (256, 32), 0)
        column = lax.broadcasted_iota(jnp.int32, (256, 32), 1)
        spread = jnp.where(row // 8 == column, 1.0, 0.0).astype(BF16)
        rows = dot_nt(spread, weight[...]).astype(BF16)
        row = lax.broadcasted_iota(jnp.int32, (256, 256), 0)
        column = lax.broadcasted_iota(jnp.int32, (256, 256), 1)
        left_c[...] = jnp.where(row % 8 == column % 8, dot_nt(rows, spread), 0.0).astype(BF16)

    for xg in range(4):
        cols = []
        for z2 in range(2):
            rows = field[0, :, z2, xg * 16 : (xg + 1) * 16, :].astype(F32)
            cols.append(rows.reshape(32, 2, 8, 128))
        halves = []
        for half in range(2):
            block = jnp.concatenate([c[:, half].reshape(256, 128) for c in cols], axis=1)
            halves.append(dot(left_c[...], block.astype(BF16)))
        for z2 in range(2):
            parts = [h[:, z2 * 128 : (z2 + 1) * 128].reshape(32, 1, 8, 128) for h in halves]
            both = jnp.concatenate(parts, axis=1).reshape(32, 16, 128)
            out[0, :, z2, xg * 16 : (xg + 1) * 16, :] = both.astype(BF16)


def local_mix(field, weight):
    plane = pl.BlockSpec((1, 32, 2, 64, 128), lambda i: (0, 0, i, 0, 0))
    return call(
        local_kernel,
        4,
        [plane, whole((32, 32))],
        plane,
        jax.ShapeDtypeStruct(field.shape, BF16),
        [pltpu.VMEM((256, 256), BF16)],
        1 << 31,
        "local_mix",
        60,
    )(field, weight)


def spread_kernel(weight, order, order_t, out):
    rows = []
    for b2 in range(2):
        for a2 in range(2):
            r = b2 * 2 + a2
            flat = weight[a2, b2].reshape(256, 32).astype(BF16)
            rows.append(dot(flat, order[r * 32 : (r + 1) * 32, :]).astype(BF16))
    for k in range(8):
        block = jnp.concatenate([v[k * 32 : (k + 1) * 32] for v in rows], axis=0)
        out[k] = dot(order_t[...], block).astype(BF16)


def spread_weights(weight, order, order_t):
    return call(
        spread_kernel,
        4,
        [pl.BlockSpec((2, 2, 8, 32, 32), lambda i: (0, 0, i, 0, 0)), whole((128, 128)), whole((128, 128))],
        pl.BlockSpec((8, 128, 128), lambda i: (i, 0, 0)),
        jax.ShapeDtypeStruct((32, 128, 128), BF16),
        [],
        1 << 28,
        "spread_weights",
        16,
    )(weight, order, order_t)


def z_modes(received, left_z, spectrum, pieces=()):
    low_half = lax.broadcasted_iota(jnp.int32, (32, 128), 1) < 64
    for pair in range(8):
        if pieces and pair % 2 == 0:
            pieces[pair // 2].wait()
        both = [received[s * 128 : (s + 1) * 128, :] for s in (2 * pair, 2 * pair + 1)]
        product = dot(left_z, jnp.concatenate(both, axis=1))
        for odd in range(2):
            p = product[:, odd * 128 : (odd + 1) * 128]
            stay = jnp.where(low_half, p[0:32], p[96:128])
            move = jnp.where(low_half, p[64:96], p[32:64])
            spectrum[pl.ds(2 * pair + odd, 32, stride=16), :] = stay + pltpu.roll(move, 64, axis=1)


def mix_kernel(received, weights, left_z, right_z, out, kept, buffer, spectrum, mixed, sems):
    pieces = []
    for i in range(4):
        rows = pl.ds(i * 512, 512)
        pieces.append(pltpu.make_async_copy(received.at[rows], buffer.at[rows], sems.at[i]))
    for piece in pieces:
        piece.start()
    z_modes(buffer, left_z[...], spectrum, pieces)
    kept[...] = spectrum[...].astype(BF16)
    for k in range(32):
        rows = slice(k * 16, (k + 1) * 16)
        mixed[rows, :] = dot(spectrum[rows, :].astype(BF16), weights[k])
    low_half = lax.broadcasted_iota(jnp.int32, (32, 128), 1) < 64
    for pair in range(8):
        blocks = []
        for s in (2 * pair, 2 * pair + 1):
            y = mixed[pl.ds(s, 32, stride=16), :]
            turned = pltpu.roll(y, 64, axis=1)
            stack = [
                jnp.where(low_half, y, 0.0),
                jnp.where(low_half, 0.0, turned),
                jnp.where(low_half, turned, 0.0),
                jnp.where(low_half, 0.0, y),
            ]
            blocks.append(jnp.concatenate(stack, axis=0).astype(BF16))
        product = dot(right_z[...], jnp.concatenate(blocks, axis=1)).astype(BF16)
        for odd in range(2):
            s = 2 * pair + odd
            out[s * 128 : (s + 1) * 128, :] = product[:, odd * 128 : (odd + 1) * 128]


def mix(received, weights, left_z, right_z):
    return call(
        mix_kernel,
        1,
        [outside(), whole((32, 128, 128)), whole((128, 128)), whole((128, 128))],
        [whole((2048, 128)), whole((512, 128))],
        [jax.ShapeDtypeStruct((2048, 128), BF16), jax.ShapeDtypeStruct((512, 128), BF16)],
        [
            pltpu.VMEM((2048, 128), BF16),
            pltpu.VMEM((512, 128), F32),
            pltpu.VMEM((512, 128), F32),
            pltpu.SemaphoreType.DMA((4,)),
        ],
        1 << 34,
        "mix_modes",
        16,
    )(received, weights, left_z, right_z)


def gelu_pull(v, cot):
    k = 0.7978845608028654
    square = v * v
    t = jnp.tanh(v * (square * low(k * 0.044715) + low(k)))
    slope = v * (square * low(3.0 * k * 0.044715) + low(k))
    one = low(1.0)
    return (one + t) * (one + (one - t) * slope) * cot


def low(value):
    return jnp.asarray(value, BF16)


def middle_kernel(
    received, local, cot, half_x, right_x, left_y, right_y, out, coefficients, planar, spectral, modes
):
    for pair in range(8):
        both = received[:, pair].astype(F32).reshape(16, 2, 8, 128)
        tiles = [both[:, odd].reshape(128, 128).T.reshape(2, 8, 8, 128) for odd in range(2)]
        coefficients[:, :, pair] = jnp.concatenate(tiles, axis=2).astype(BF16)

    def inverse_x(step):
        for i in range(2):
            halves = [coefficients[z2, step * 2 + i].reshape(128, 128) for z2 in range(2)]
            rows = slice(i * 256, (i + 1) * 256)
            spectral[rows, :] = dot(right_x[...], jnp.concatenate(halves, axis=1)).astype(BF16)

    def some(step, carry):
        store_modes(planar, modes, half_x[...], jnp.maximum(step - 1, 0) * 2)
        channels = pl.ds(step * 8, 8)
        planes = []
        for z2 in range(2):
            pre = dot(spectral[:, z2 * 128 : (z2 + 1) * 128], left_y[...]).astype(BF16)
            for zq in range(4):
                z = zq * 2 + z2
                v = pre[:, zq * 128 : (zq + 1) * 128] + local[0, channels, z].reshape(512, 128)
                planes.append(gelu_pull(v, cot[0, channels, z].reshape(512, 128)))
        inverse_x(jnp.minimum(step + 1, 3))
        modes[...] = y_modes(right_y[...], planes)
        return carry

    inverse_x(0)
    modes[...] = jnp.zeros((512, 256), BF16)
    lax.fori_loop(0, 4, some, 0)
    store_modes(planar, modes, half_x[...], 6)
    store_messages(planar, out)


def middle(received, local, cot, half_x, right_x, left_y, right_y):
    return call(
        middle_kernel,
        1,
        [
            whole(MESSAGES),
            resident(),
            resident(),
            whole((128, 256)),
            whole((256, 128)),
            whole((128, 512)),
            whole((512, 128)),
        ],
        whole(MESSAGES),
        jax.ShapeDtypeStruct(MESSAGES, BF16),
        [
            pltpu.VMEM((2, 8, 8, 16, 128), BF16),
            pltpu.VMEM(PLANAR, F32),
            pltpu.VMEM((512, 256), BF16),
            pltpu.VMEM((512, 256), BF16),
        ],
        1 << 32,
        "gelu_gradient",
        32,
    )(received.reshape(MESSAGES), local, cot, half_x, right_x, left_y, right_y).reshape(2048, 128)


STEP = 16


def update_kernel(
    received, kept, left_z, order_t, weight, moment, second, new_weight, new_moment, new_second, spectrum, results, sems
):
    z_modes(received, left_z[...], spectrum)

    def copies(step):
        some = pl.ds(step * STEP, STEP)
        return [
            pltpu.make_async_copy(results.at[i, :, :, some], target.at[:, :, some], sems.at[i, step])
            for i, target in enumerate((new_weight, new_moment, new_second))
        ]

    for step in range(32 // STEP):
        rows = slice(step * STEP * 16, (step + 1) * STEP * 16)
        left = dot(kept[rows, :], order_t[...]).T.astype(BF16)
        right = dot(spectrum[rows, :].astype(BF16), order_t[...]).astype(BF16)
        zero = jnp.zeros((16, 128), BF16)
        columns = []
        for i in range(STEP):
            tiles = [zero] * STEP
            tiles[i] = right[i * 16 : (i + 1) * 16]
            columns.append(jnp.concatenate(tiles, axis=0))
        product = dot(left, jnp.concatenate(columns, axis=1))
        for i in range(STEP):
            k = step * STEP + i
            for b2 in range(2):
                for a2 in range(2):
                    r = b2 * 2 + a2
                    block = product[r * 32 : (r + 1) * 32, i * 128 : (i + 1) * 128]
                    if r:
                        block = pltpu.roll(block, 128 - 32 * r, axis=1)
                    grad = block[:, :32]
                    first = beta_one * moment[a2, b2, k] + (1.0 - beta_one) * grad
                    square = beta_two * second[a2, b2, k] + (1.0 - beta_two) * grad * grad
                    results[1, a2, b2, k] = first
                    results[2, a2, b2, k] = square
                    second_hat = square * (1.0 / (1.0 - beta_two**adam_step))
                    root = second_hat * lax.rsqrt(second_hat)
                    scaled = first * (learn_rate / (1.0 - beta_one**adam_step))
                    kept_weight = weight[a2, b2, k] * (1.0 - learn_rate * decay_rate)
                    results[0, a2, b2, k] = kept_weight - scaled / (root + adam_eps)
        for copy in copies(step):
            copy.start()
    for step in range(32 // STEP):
        for copy in copies(step):
            copy.wait()


def update(received, kept, left_z, order_t, weight, moment, second):
    return call(
        update_kernel,
        1,
        [whole((2048, 128)), whole((512, 128)), whole((128, 128)), whole((128, 128))] + [resident()] * 3,
        [outside()] * 3,
        [jax.ShapeDtypeStruct(weight.shape, F32)] * 3,
        [
            pltpu.VMEM((512, 128), F32),
            pltpu.VMEM((3,) + weight.shape, F32),
            pltpu.SemaphoreType.DMA((3, 32 // STEP)),
        ],
        1 << 28,
        "adam_update",
        24,
    )(received, kept, left_z, order_t, weight, moment, second)


def exchange(messages):
    return lax.all_to_all(messages, ("dp", "mp"), split_axis=0, concat_axis=0, tiled=True)


def body(field, cotangent, spectral_weight, first_moment, second_moment, local_weight):
    left_x, right_x, half_x, right_y, left_y, left_z, right_z, order, order_t = constants()
    received = exchange(forward(field, left_x, right_y))
    local = local_mix(field, local_weight)
    spread = spread_weights(spectral_weight, order, order_t)
    received, local, spread = lax.optimization_barrier((received, local, spread))
    mixed, kept = mix(received, spread, left_z, right_z)
    received = exchange(mixed)
    received = exchange(middle(received, local, cotangent, half_x, right_x, left_y, right_y))
    return tuple(update(received, kept, left_z, order_t, spectral_weight, first_moment, second_moment))


def solution(mesh):
    spread = P("dp", None, "mp", None, None)
    modes = P("mp", "dp", None, None, None)
    return jax.shard_map(
        body,
        mesh=mesh,
        in_specs=(spread, spread, modes, modes, modes, P()),
        out_specs=(modes, modes, modes),
        check_vma=False,
    )
```
